32 devices in a mesh: req: 8 (over z, y), blk: 4 (over x, core).
Axes of the slice: x: 2, y: 2, z: 4, core: 2. Of those that a mesh axis runs over, the one named last changes fastest.
Arguments:
- step_inputs: bfloat16 [2, 512, 2560], P(None, 'req', 'blk'), may hold values from -6 to 6
- attention_gain: float32 [2560], replicated, may hold values from 0.25 to 1.75
- query_weight: bfloat16 [2560, 2560], P(None, 'blk'), may hold values from -0.3125 to 0.3125
- key_value_weight: bfloat16 [2560, 1024], P(None, 'blk'), may hold values from -0.125 to 0.125
- output_weight: bfloat16 [2560, 2560], P(None, 'blk'), may hold values from -0.125 to 0.125
- prompt_cache: bfloat16 [8, 48, 128, 1024], P('req', 'blk'), may hold values from -102 to 102
- page_table: int32 [8, 4, 12], P(None, 'blk'), may hold values from 0 to 11, each once within a row
- cache_lengths: int32 [8], replicated, may hold values from 1 to 6144, 24576 in all
- migration: int32 [8], replicated, may hold values from 0 to 7, each once
- parents: int32 [1, 512], P(None, 'req'), may hold values from 0 to 7
- routes: int32 [2, 512, 6], P(None, 'req'), may hold values from 0 to 63, all different within a row; in each aligned block of 64 rows (0 to 63, 64 to 127, ..., all dimensions but the last counted through in order) at most 16 rows name the same one
- feedforward_gain: float32 [2560], replicated, may hold values from 0.25 to 1.75
- router_weight: bfloat16 [2560, 64], replicated, may hold values from -0.125 to 0.125
- expert_gate: bfloat16 [64, 2560, 1536], P(('req', 'blk')), may hold values from -0.125 to 0.125
- expert_up: bfloat16 [64, 2560, 1536], P(('req', 'blk')), may hold values from -0.125 to 0.125
- expert_down: bfloat16 [64, 1536, 2560], P(('req', 'blk')), may hold values from -0.15625 to 0.15625
- shared_gate: bfloat16 [2560, 3072], P(None, 'blk'), may hold values from -0.125 to 0.125
- shared_up: bfloat16 [2560, 3072], P(None, 'blk'), may hold values from -0.125 to 0.125
- shared_down: bfloat16 [3072, 2560], P('blk'), may hold values from -0.15625 to 0.15625
Outputs:
- layer_outputs: bfloat16 [2, 512, 2560], P(None, 'req', 'blk')
The draws below stay inside these ranges and needn't reach their ends.
Inputs may be any that keep to these rules, and one draw needn't show every extreme that they name: `routes`: in each step the 64 rows of one device along req name any one expert at most 16 times. `migration`: A permutation of the slots. Each page_table[g, c] is a permutation.
All inputs are finite; a program needn't handle non-finite values.
Results may differ from the reference program's by a relative error of at most 0.018.
The reference program's roundings to bfloat16 on the way count: a program that leaves them out, or rounds other values in their place, can miss the bound.
Values may be sent and summed in bfloat16 or wider, within the bound.
A program may use at most 128 MiB of HBM per device.

```python
import math
import jax
import jax.numpy as jnp
import numpy as np
from jax import lax

D = 2560
QUERY_HEADS = 20
KEY_VALUE_HEADS = 4
HEAD_WIDTH = 128
E = 64
FFE = 1536
TOPK = 6
SH = 3072
BEAMS = 8
STEPS = 2
PAGE = 128
CAP = 16
GR = 8
PROMPT_LIMIT = 6144
G = 8
ROWS_DEV = 64
BEAM_ROWS = 512
KEY_VALUE_WIDTH = 1024
PAGES = 48
PAGE_COLS = 4
PAGES_LOC = 12
SPLIT = 1
FQ = 1536
N_REQ = 8


def draw_prompt_cache(key, part):
    cache_shape = (G, PAGE_COLS * PAGES_LOC, PAGE, KEY_VALUE_WIDTH)
    normal_key = jax.random.fold_in(key, 0)
    values = jnp.clip(jax.random.normal(normal_key, cache_shape, jnp.float32), -6.0, 6.0)
    return values.astype(jnp.bfloat16)


def with_ends(drawn, key, smallest, top_value):
    extent = drawn.shape
    place = [jax.random.randint(jax.random.fold_in(key, axis), (), 0, extent[axis]) for axis in range(len(extent))]
    drawn = drawn.at[tuple(place)].set(smallest)
    longest = extent.index(max(extent))
    place[longest] = (place[longest] + 1) % extent[longest]
    return drawn.at[tuple(place)].set(top_value)


def with_spikes(entries, key, source, target, parts, factor):
    owner, partner = [(jnp.arange(entries.shape[axis_at]) // (entries.shape[axis_at] // parts)).reshape([-1 if axis == axis_at else 1 for axis in range(entries.ndim)]) for axis_at in (source, target)]
    chosen = jax.random.permutation(key, parts)[partner]
    strong = (owner == chosen) | (owner == (partner + parts // 2) % parts)
    return jnp.where(strong, factor * entries, entries)


def steps_of(key, dims, cuts, smallest, high):
    factor_of, own = 1.0, jax.random.fold_in(key, 6)
    for dim, parts in cuts:
        draws = jnp.exp(jax.random.uniform(jax.random.fold_in(own, dim), (parts,), jnp.float32, smallest / len(cuts), high / len(cuts)))
        factor_of = factor_of * jnp.repeat(draws, dims[dim] // parts).reshape([-1 if axis == dim else 1 for axis in range(len(dims))])
    return factor_of


def profile(amount, total, limit, skew):
    weights = [(1 << 20) // math.isqrt(grade ** skew) + 1 for grade in range(2, amount + 1)]
    spare, given = total - limit - (amount - 1), [1] * (amount - 1)
    while spare > 0:
        free = [i for i in range(amount - 1) if given[i] < limit]
        mass, left = sum([weights[i] for i in free]), spare
        for i in free:
            extra = min(limit - given[i], max(1, left * weights[i] // mass), spare)
            given[i] = given[i] + extra
            spare = spare - extra
    return np.array([limit] + given)


def uneven(own_key, number_of, total, most, skew):
    if number_of == 2:
        one = jax.random.randint(own_key, (), max(1, total - most), min(most, total - 1) + 1)
        return jnp.stack([one, total - one])
    sizes = jnp.asarray(profile(number_of, total, most, skew), jnp.int32)
    couples = (number_of - 1) // 2
    giver, receiver = sizes[1:1 + 2 * couples:2], sizes[2:2 + 2 * couples:2]
    slack = jnp.minimum(giver - 1, most - receiver)
    moved = jax.random.randint(jax.random.fold_in(own_key, 1), (couples,), 0, 1 << 20) % (slack + 1)
    sizes = sizes.at[1:1 + 2 * couples:2].set(giver - moved).at[2:2 + 2 * couples:2].set(receiver + moved)
    return sizes[jax.random.permutation(jax.random.fold_in(own_key, 2), number_of)]


def routed_block(own_key, own, number, rows, number_of, top, reach, slope):
    ranking = jax.random.permutation(own_key, number_of)
    heavy_load, usual = shares(number_of, rows * top, reach, slope, True), shares(number_of, rows * top, reach, slope, False)
    places = jnp.arange(number_of)

    def named(tallies, offset_by):
        used = int((tallies > 0).sum())
        fixed = max(1, used // 4)
        shifted = fixed + (places - fixed + offset_by * (used - fixed)) % max(1, number_of - fixed)
        return jnp.zeros((number_of,), jnp.int32).at[ranking[jnp.where(places < fixed, places, shifted)]].set(jnp.asarray(tallies, jnp.int32))

    tallies = jnp.where(number % 4 == 0, named(heavy_load, number // 4), named(usual, number - number // 4 - 1))
    mixed = jax.random.permutation(jax.random.fold_in(own, 3), number_of)
    giver, receiver = mixed[0:number_of // 2 * 2:2], mixed[1:number_of // 2 * 2:2]
    slack = jnp.minimum(tallies[giver] - 1, reach - tallies[receiver]) // 2
    slack = jnp.where((giver == ranking[0]) | (receiver == ranking[0]) | (tallies[receiver] == 0), 0, jnp.maximum(slack, 0))
    shifted = jax.random.randint(jax.random.fold_in(own, 4), (number_of // 2,), 0, 1 << 20) % (slack + 1)
    tallies = tallies.at[giver].add(-shifted).at[receiver].add(shifted)
    labels = jnp.searchsorted(jnp.cumsum(tallies), jnp.arange(rows * top), side="right").astype(jnp.int32)
    listing = labels.reshape(top, rows).T
    listing = listing[jax.random.permutation(jax.random.fold_in(own, 1), rows)]
    offset_by = jax.random.randint(jax.random.fold_in(own, 2), (rows, 1), 0, top)
    return jnp.take_along_axis(listing, (jnp.arange(top)[None, :] + offset_by) % top, axis=1)


def shares(number_of, total, most, lean, full):
    weights = [(1 << 20) // math.isqrt(grade ** lean) + 1 for grade in range(1, number_of + 1)]
    largest = most if full else min(most, max(-(-total // number_of), total * weights[0] // sum(weights)))
    least = 1 if total - largest >= number_of - 1 else 0
    counts, surplus = [largest] + [least] * (number_of - 1), total - largest - least * (number_of - 1)
    while surplus > 0:
        free = [i for i in range(1, number_of) if counts[i] < largest] or [i for i in range(1, number_of) if counts[i] < most]
        mass, remaining = sum([weights[i] for i in free]), surplus
        for i in free:
            more = min(most - counts[i], max(1, remaining * weights[i] // mass), surplus)
            counts[i] = counts[i] + more
            surplus = surplus - more
    return np.array(counts)


def scatter_about(key, extent, scale, limit, cuts=(), kind=jnp.bfloat16):
    entries = jax.random.normal(key, extent, jnp.float32) * scale
    if len(cuts) > 0:
        entries = steps_of(key, extent, cuts, -0.22, 0.18) * entries
    return jnp.clip(entries, min=-limit, max=limit).astype(kind)


def noise_with(stream_key, dims, scale, most, cuts, heavy, held_as=jnp.bfloat16):
    result = scale * jax.random.normal(stream_key, dims, jnp.float32)
    if cuts:
        result = result * steps_of(stream_key, dims, cuts, -0.22, 0.18)
    return jnp.clip(with_spikes(result, jax.random.fold_in(stream_key, 3), *heavy), -most, most).astype(held_as)


def setup_inputs(seed: int = 0) -> dict:
    seeds = jax.random.split(jax.random.key(seed), 20)
    step_inputs = scatter_about(seeds[0], (STEPS, BEAM_ROWS, D), 1.0, 6.0, ((1, 8), (2, 4)))
    attention_gain = jnp.clip(1.0 + 0.15 * jax.random.normal(seeds[1], (D,), jnp.float32), 0.25, 1.75)
    query_weight = scatter_about(seeds[2], (D, QUERY_HEADS * HEAD_WIDTH), (D // 6) ** -0.5, 0.3125, ((1, 4),))
    key_value_weight = scatter_about(seeds[3], (D, KEY_VALUE_WIDTH), D ** -0.5, 0.125, ((1, 4),))
    output_weight = scatter_about(seeds[4], (QUERY_HEADS * HEAD_WIDTH, D), (QUERY_HEADS * HEAD_WIDTH) ** -0.5, 0.125, ((1, 4),))
    prompt_cache = draw_prompt_cache(jax.random.fold_in(seeds[19], 71), 0)
    page_table = jax.vmap(lambda own: jax.random.permutation(own, PAGES_LOC))(jax.random.split(seeds[6], G * PAGE_COLS)).reshape((G, PAGE_COLS, PAGES_LOC)).astype(jnp.int32)
    cache_lengths = uneven(seeds[7], G, G * PROMPT_LIMIT // 2, PROMPT_LIMIT, 2).astype(jnp.int32)
    migration = jax.random.permutation(seeds[8], G).astype(jnp.int32)
    parents = with_ends(jax.random.randint(seeds[9], (STEPS - 1, BEAM_ROWS), 0, BEAMS), jax.random.fold_in(seeds[9], 1), 0, BEAMS - 1).astype(jnp.int32)
    routes_keys = jax.random.split(jax.random.fold_in(seeds[10], 1), STEPS * BEAM_ROWS // ROWS_DEV)
    routes_turns = jax.random.permutation(jax.random.fold_in(seeds[10], 3), STEPS * BEAM_ROWS // ROWS_DEV)
    routes = jax.vmap(lambda own, number: routed_block(jax.random.fold_in(seeds[10], 2), own, number, ROWS_DEV, E, TOPK, CAP, 2))(routes_keys, routes_turns).reshape((STEPS, BEAM_ROWS, TOPK))
    feedforward_gain = jnp.clip(1.0 + 0.15 * jax.random.normal(seeds[11], (D,), jnp.float32), 0.25, 1.75)
    router_weight = scatter_about(seeds[12], (D, E), D ** -0.5, 0.125)
    expert_gate = scatter_about(seeds[13], (E * SPLIT, D, FQ), D ** -0.5, 0.125, ((0, 32),))
    expert_up = scatter_about(seeds[14], (E * SPLIT, D, FQ), D ** -0.5, 0.125, ((0, 32),))
    expert_down = scatter_about(seeds[15], (E * SPLIT, FQ, D), FFE ** -0.5, 0.15625, ((0, 32),))
    shared_gate = scatter_about(seeds[16], (D, SH), D ** -0.5, 0.125, ((1, 4),))
    shared_up = scatter_about(seeds[17], (D, SH), D ** -0.5, 0.125, ((1, 4),))
    shared_down = noise_with(seeds[18], (SH, D), SH ** -0.5, 0.15625, ((0, 4),), (0, 1, 4, 2.0))
    return dict(step_inputs=step_inputs, attention_gain=attention_gain, query_weight=query_weight, key_value_weight=key_value_weight, output_weight=output_weight, prompt_cache=prompt_cache, page_table=page_table, cache_lengths=cache_lengths, migration=migration, parents=parents, routes=routes, feedforward_gain=feedforward_gain, router_weight=router_weight, expert_gate=expert_gate, expert_up=expert_up, expert_down=expert_down, shared_gate=shared_gate, shared_up=shared_up, shared_down=shared_down)


epsilon = 1e-05
rope_base = 500000.0
masked_floor = -1e+30

def norm_rows(values, gain):
    as_float = values.astype(jnp.float32)
    inverse = lax.rsqrt(lax.optimization_barrier(jnp.mean(as_float * as_float, axis=-1, keepdims=True)) + epsilon)
    return (as_float * inverse * gain).astype(jnp.bfloat16)

def apply_rotary(vectors, position_list):
    half_width = vectors.shape[-1] // 2
    frequency = rope_base ** (-2.0 * jnp.arange(half_width, dtype=jnp.float32) / vectors.shape[-1])
    angles = position_list.astype(jnp.float32)[:, None, None] * frequency
    cosine_part = jnp.cos(angles)
    sine_part = jnp.sin(angles)
    leading = vectors[..., :half_width]
    trailing = vectors[..., half_width:]
    return jnp.concatenate([leading * cosine_part - trailing * sine_part, trailing * cosine_part + leading * sine_part], axis=-1)

def reference(step_inputs, attention_gain, query_weight, key_value_weight, output_weight, prompt_cache, page_table, cache_lengths, migration, parents, routes, feedforward_gain, router_weight, expert_gate, expert_up, expert_down, shared_gate, shared_up, shared_down):
    group_of_rows = GR * BEAMS
    heads_per_group = QUERY_HEADS // KEY_VALUE_HEADS
    scaling = HEAD_WIDTH ** (-0.5)
    logical = jnp.arange(PAGES, dtype=jnp.int32)
    column_of = logical % PAGE_COLS
    local_of = logical // PAGE_COLS
    physical = column_of[None, :] * PAGES_LOC + page_table[:, column_of, local_of]
    ordered = jax.vmap(lambda pages, ordering: pages[ordering])(prompt_cache, physical)
    ordered = ordered.reshape(G, PROMPT_LIMIT, KEY_VALUE_WIDTH)
    inverse = jnp.zeros((G,), jnp.int32).at[migration].set(jnp.arange(G, dtype=jnp.int32))
    slot_lengths = cache_lengths[inverse]
    row_ids = jnp.arange(BEAM_ROWS, dtype=jnp.int32)
    slot_of_row = row_ids // group_of_rows
    tail_entries = []
    results = []
    for step_index in range(STEPS):
        current = step_inputs[step_index]
        if step_index > 0:
            parent_rows = row_ids // BEAMS * BEAMS + parents[step_index - 1]
            tail_entries = [(entry_pair[0][parent_rows], entry_pair[1][parent_rows]) for entry_pair in tail_entries]
        normed_x = norm_rows(current, attention_gain)
        projected_q = jnp.dot(normed_x, query_weight, preferred_element_type=jnp.float32).astype(jnp.bfloat16)
        key_value_projected = jnp.dot(normed_x, key_value_weight, preferred_element_type=jnp.float32).astype(jnp.bfloat16)
        position_list = slot_lengths[slot_of_row] + step_index
        query_vectors = apply_rotary(projected_q.astype(jnp.float32).reshape(BEAM_ROWS, QUERY_HEADS, HEAD_WIDTH), position_list).astype(jnp.bfloat16)
        step_keys = apply_rotary(key_value_projected[:, :KEY_VALUE_HEADS * HEAD_WIDTH].astype(jnp.float32).reshape(BEAM_ROWS, KEY_VALUE_HEADS, HEAD_WIDTH), position_list).astype(jnp.bfloat16).reshape(BEAM_ROWS, KEY_VALUE_HEADS * HEAD_WIDTH)
        step_values = key_value_projected[:, KEY_VALUE_HEADS * HEAD_WIDTH:]
        tail_entries = tail_entries + [(step_keys, step_values)]
        recent_keys = jnp.stack([entry_pair[0] for entry_pair in tail_entries], axis=1)
        recent_values = jnp.stack([entry_pair[1] for entry_pair in tail_entries], axis=1)
        tail_length = len(tail_entries)

        def one_group(slot):
            owner = inverse[slot]
            cache_entries = lax.dynamic_index_in_dim(ordered, owner, 0, keepdims=False)
            heads_of_keys = cache_entries[:, :KEY_VALUE_HEADS * HEAD_WIDTH].reshape(PROMPT_LIMIT, KEY_VALUE_HEADS, HEAD_WIDTH).astype(jnp.float32)
            heads_of_values = cache_entries[:, KEY_VALUE_HEADS * HEAD_WIDTH:].reshape(PROMPT_LIMIT, KEY_VALUE_HEADS, HEAD_WIDTH).astype(jnp.float32)
            beginning_row = slot * group_of_rows
            grouped_rows = lax.dynamic_slice_in_dim(query_vectors, beginning_row, group_of_rows, 0).astype(jnp.float32).reshape(group_of_rows, KEY_VALUE_HEADS, heads_per_group, HEAD_WIDTH)
            beam_keys = lax.dynamic_slice_in_dim(recent_keys, beginning_row, group_of_rows, 0).astype(jnp.float32).reshape(group_of_rows, tail_length, KEY_VALUE_HEADS, HEAD_WIDTH)
            beam_values = lax.dynamic_slice_in_dim(recent_values, beginning_row, group_of_rows, 0).astype(jnp.float32).reshape(group_of_rows, tail_length, KEY_VALUE_HEADS, HEAD_WIDTH)
            cache_scores = jnp.einsum('rkqd,skd->rkqs', grouped_rows, heads_of_keys) * scaling
            tail_scores = jnp.einsum('rkqd,rtkd->rkqt', grouped_rows, beam_keys) * scaling
            valid = jnp.arange(PROMPT_LIMIT, dtype=jnp.int32) < slot_lengths[slot]
            largest = jnp.maximum(lax.optimization_barrier(jnp.max(jnp.where(valid, cache_scores, masked_floor), axis=-1)), lax.optimization_barrier(jnp.max(tail_scores, axis=-1)))
            cache_probs = jnp.where(valid, jnp.exp(cache_scores - largest[..., None]), 0.0)
            tail_probs = jnp.exp(tail_scores - largest[..., None])
            denominators = lax.optimization_barrier(jnp.sum(cache_probs, axis=-1)) + lax.optimization_barrier(jnp.sum(tail_probs, axis=-1))
            rounded_cache = lax.optimization_barrier(cache_probs.astype(jnp.bfloat16)).astype(jnp.float32)
            rounded_tail = lax.optimization_barrier(tail_probs.astype(jnp.bfloat16)).astype(jnp.float32)
            weighted_values = jnp.einsum('rkqs,skd->rkqd', rounded_cache, heads_of_values) + jnp.einsum('rkqt,rtkd->rkqd', rounded_tail, beam_values)
            return (weighted_values / denominators[..., None]).astype(jnp.bfloat16).reshape(group_of_rows, QUERY_HEADS * HEAD_WIDTH)
        heads = lax.map(one_group, jnp.arange(G, dtype=jnp.int32)).reshape(BEAM_ROWS, QUERY_HEADS * HEAD_WIDTH)
        attended = (current.astype(jnp.float32) + jnp.dot(heads, output_weight, preferred_element_type=jnp.float32)).astype(jnp.bfloat16)
        normed_h = norm_rows(attended, feedforward_gain)
        logits = jnp.dot(normed_h, router_weight, preferred_element_type=jnp.float32)
        chosen = routes[step_index]
        raised = jnp.exp(jnp.take_along_axis(logits, chosen, axis=1))
        gate_weights = raised / lax.optimization_barrier(jnp.sum(raised, axis=1, keepdims=True))
        flat_routes = chosen.reshape(N_REQ, ROWS_DEV * TOPK)
        one_hot = (flat_routes[:, :, None] == jnp.arange(E, dtype=jnp.int32)[None, None, :]).astype(jnp.int32)
        ranks = lax.optimization_barrier(jnp.sum((jnp.cumsum(one_hot, axis=1) - 1) * one_hot, axis=2))
        slot_index = (jnp.arange(N_REQ, dtype=jnp.int32)[:, None] * CAP + ranks).reshape(BEAM_ROWS, TOPK)
        row_numbers = jnp.repeat(row_ids, TOPK)
        table = jnp.zeros((E, N_REQ * CAP), jnp.int32).at[chosen.reshape(-1), slot_index.reshape(-1)].set(row_numbers)
        filled = jnp.zeros((E, N_REQ * CAP), jnp.bool_).at[chosen.reshape(-1), slot_index.reshape(-1)].set(True)

        def one_expert(expert):
            members = jnp.where(filled[expert][:, None], normed_h[table[expert]], jnp.zeros((), jnp.bfloat16))
            summed = jnp.zeros((N_REQ * CAP, D), jnp.float32)
            for block_index in range(SPLIT):
                weight_index = expert * SPLIT + block_index
                gate_part = jnp.dot(members, expert_gate[weight_index], preferred_element_type=jnp.float32)
                up_part = jnp.dot(members, expert_up[weight_index], preferred_element_type=jnp.float32)
                hidden = (jax.nn.silu(gate_part) * up_part).astype(jnp.bfloat16)
                partial_value = jnp.dot(hidden, expert_down[weight_index], preferred_element_type=jnp.float32).astype(jnp.bfloat16)
                summed = summed + lax.optimization_barrier(partial_value).astype(jnp.float32)
            return summed
        expert_out = lax.map(one_expert, jnp.arange(E, dtype=jnp.int32))
        gathered = expert_out[chosen, slot_index]
        routed = lax.optimization_barrier(jnp.sum(gate_weights[..., None] * gathered, axis=1))
        shared_act = (jax.nn.silu(jnp.dot(normed_h, shared_gate, preferred_element_type=jnp.float32)) * jnp.dot(normed_h, shared_up, preferred_element_type=jnp.float32)).astype(jnp.bfloat16)
        shared = jnp.dot(shared_act, shared_down, preferred_element_type=jnp.float32)
        results.append((attended.astype(jnp.float32) + routed + shared).astype(jnp.bfloat16))
    return jnp.stack(results, axis=0)
```

```python
import functools

import jax
import jax.numpy as jnp
from jax import lax
from jax.experimental import pallas as pl
from jax.experimental.pallas import tpu as pltpu
from jax.sharding import PartitionSpec as P

QUERY_HEADS = 20
KEY_VALUE_HEADS = 4
HEAD_WIDTH = 128
E = 64
FFE = 1536
TOPK = 6
BEAMS = 8
CAP = 16
GROUP = QUERY_HEADS // KEY_VALUE_HEADS

epsilon = 1e-05
rope_base = 500000.0
masked_floor = -1e30
MIB = 1 << 20


def push_kernel(axis, n, count, gather, *refs):
    ins, outs = refs[:count], refs[count : 2 * count]
    send_sem, recv_sem, local_sem = refs[2 * count :]
    me = lax.axis_index(axis)
    barrier = pltpu.get_barrier_semaphore()
    for k in range(1, n):
        pl.semaphore_signal(
            barrier,
            inc=1,
            device_id={axis: lax.rem(me + k, n)},
            device_id_type=pl.DeviceIdType.MESH,
        )
    pl.semaphore_wait(barrier, n - 1)
    copies = []
    for k in range(1, n):
        to = lax.rem(me + k, n)
        for i in range(count):
            copy = pltpu.make_async_remote_copy(
                src_ref=ins[i] if gather else ins[i].at[to],
                dst_ref=outs[i].at[me],
                send_sem=send_sem.at[i, k],
                recv_sem=recv_sem.at[i, k],
                device_id={axis: to},
                device_id_type=pl.DeviceIdType.MESH,
            )
            copy.start()
            copies.append(copy)
    own = []
    for i in range(count):
        copy = pltpu.make_async_copy(
            ins[i] if gather else ins[i].at[me], outs[i].at[me], local_sem.at[i]
        )
        copy.start()
        own.append(copy)
    for copy in own:
        copy.wait()
    for copy in copies:
        copy.wait()


def push(arrays, axis, collective_id, gather=False):
    n = lax.axis_size(axis)
    count = len(arrays)
    shapes = [
        jax.ShapeDtypeStruct(((n,) + a.shape) if gather else a.shape, a.dtype) for a in arrays
    ]
    return pl.pallas_call(
        functools.partial(push_kernel, axis, n, count, gather),
        out_shape=shapes,
        in_specs=[pl.BlockSpec(memory_space=pl.ANY)] * count,
        out_specs=[pl.BlockSpec(memory_space=pl.ANY)] * count,
        scratch_shapes=[
            pltpu.SemaphoreType.DMA((count, n)),
            pltpu.SemaphoreType.DMA((count, n)),
            pltpu.SemaphoreType.DMA((count,)),
        ],
        compiler_params=pltpu.CompilerParams(collective_id=collective_id, has_side_effects=True),
        name=f"push_{axis}_{collective_id}",
    )(*arrays)


def gather_columns(array, axis, collective_id):
    (blocks,) = push([array], axis, collective_id, gather=True)
    return jnp.transpose(blocks, (1, 0, 2)).reshape(array.shape[0], -1)


def permute_rows(rows, block_for, ids):
    n = lax.axis_size("req")
    pieces = rows.reshape(n, rows.shape[0] // n, rows.shape[1])
    (spread,) = push([pieces], "req", ids[0])
    (arrived,) = push([jnp.take(spread, block_for, axis=0)], "req", ids[1])
    return arrived.reshape(rows.shape)


def attention_kernel(
    tail_ref, q_ref, kv_ref, parent_ref, cos_ref, sin_ref, pos_ref, cache_ref, o_ref, lse_ref
):
    rows = q_ref.shape[0]
    scaling = HEAD_WIDTH ** (-0.5)
    key_width = KEY_VALUE_HEADS * HEAD_WIDTH
    cosines, sines = cos_ref[...], sin_ref[...]

    def rotated(block):
        block = block.astype(jnp.float32)
        half = HEAD_WIDTH // 2
        swapped = jnp.concatenate([block[:, half:], block[:, :half]], axis=1)
        return (block * cosines + swapped * sines).astype(jnp.bfloat16)

    tails_here = tail_ref[0] > 0
    valid = pos_ref[...] < tail_ref[1]
    parent = parent_ref[...]
    has_parent = jnp.sum(parent.astype(jnp.float32), axis=1, keepdims=True) > 0.5
    lse_ref[...] = jnp.full(lse_ref.shape, masked_floor, jnp.float32)
    for kv_head in range(KEY_VALUE_HEADS):
        keys_at = pl.ds(kv_head * HEAD_WIDTH, HEAD_WIDTH)
        values_at = pl.ds(key_width + kv_head * HEAD_WIDTH, HEAD_WIDTH)
        own_key = rotated(kv_ref[:, keys_at])
        own_value = kv_ref[:, values_at]
        parent_key = jnp.dot(parent, own_key, preferred_element_type=jnp.float32)
        parent_value = jnp.dot(parent, own_value, preferred_element_type=jnp.float32)
        own_key = own_key.astype(jnp.float32)
        own_value = own_value.astype(jnp.float32)
        keys = cache_ref[:, keys_at]
        values = cache_ref[:, values_at]
        for g in range(GROUP):
            head = kv_head * GROUP + g
            at = pl.ds(head * HEAD_WIDTH, HEAD_WIDTH)
            query = rotated(q_ref[:, at])
            scores = (
                lax.dot_general(
                    query, keys, (((1,), (1,)), ((), ())), preferred_element_type=jnp.float32
                )
                * scaling
            )
            query = query.astype(jnp.float32)
            own = jnp.sum(query * own_key, axis=1, keepdims=True) * scaling
            par = jnp.sum(query * parent_key, axis=1, keepdims=True) * scaling
            own = jnp.where(tails_here, own, masked_floor)
            par = jnp.where(has_parent & tails_here, par, masked_floor)
            scores = jnp.where(valid, scores, masked_floor)
            peak = jnp.maximum(jnp.max(scores, axis=1, keepdims=True), jnp.maximum(own, par))
            probs = jnp.where(valid, jnp.exp(scores - peak), 0.0)
            own = jnp.where(tails_here, jnp.exp(own - peak), 0.0)
            par = jnp.where(has_parent & tails_here, jnp.exp(par - peak), 0.0)
            total = jnp.sum(probs, axis=1, keepdims=True) + own + par
            weighted = jnp.dot(
                probs.astype(jnp.bfloat16), values, preferred_element_type=jnp.float32
            )
            weighted += own.astype(jnp.bfloat16).astype(jnp.float32) * own_value
            weighted += par.astype(jnp.bfloat16).astype(jnp.float32) * parent_value
            live = total > 0.0
            safe = jnp.where(live, total, 1.0)
            o_ref[:, at] = (weighted / safe).astype(jnp.bfloat16)
            lse_ref[:, head : head + 1] = jnp.where(live, peak + jnp.log(safe), masked_floor)


def attention_part(tail, q, kv, parent, cosines, sines, positions, cache):
    rows = q.shape[0]
    vmem = pl.BlockSpec(memory_space=pltpu.VMEM)
    return pl.pallas_call(
        attention_kernel,
        out_shape=[
            jax.ShapeDtypeStruct(q.shape, jnp.bfloat16),
            jax.ShapeDtypeStruct((rows, HEAD_WIDTH), jnp.float32),
        ],
        in_specs=[pl.BlockSpec(memory_space=pltpu.SMEM)] + [vmem] * 7,
        out_specs=[vmem] * 2,
        compiler_params=pltpu.CompilerParams(vmem_limit_bytes=40 * MIB),
        name="attention_part",
    )(tail, q, kv, parent, cosines, sines, positions, cache)


def merge_kernel(o_ref, lse_ref, out_ref):
    n = o_ref.shape[0]
    peaks = lse_ref[0]
    for b in range(1, n):
        peaks = jnp.maximum(peaks, lse_ref[b])
    scales = [jnp.exp(lse_ref[b] - peaks) for b in range(n)]
    total = scales[0]
    for b in range(1, n):
        total = total + scales[b]
    scales = [scale / total for scale in scales]
    for head in range(QUERY_HEADS):
        at = pl.ds(head * HEAD_WIDTH, HEAD_WIDTH)
        acc = o_ref[0, :, at].astype(jnp.float32) * scales[0][:, head : head + 1]
        for b in range(1, n):
            acc += o_ref[b, :, at].astype(jnp.float32) * scales[b][:, head : head + 1]
        out_ref[:, at] = acc.astype(jnp.bfloat16)


def merge(parts, lse):
    vmem = pl.BlockSpec(memory_space=pltpu.VMEM)
    return pl.pallas_call(
        merge_kernel,
        out_shape=jax.ShapeDtypeStruct(parts.shape[1:], jnp.bfloat16),
        in_specs=[vmem] * 2,
        out_specs=vmem,
        compiler_params=pltpu.CompilerParams(vmem_limit_bytes=40 * MIB),
        name="merge",
    )(parts, lse)


def norm_rows(values, gain):
    as_float = values.astype(jnp.float32)
    inverse = lax.rsqrt(jnp.mean(as_float * as_float, axis=-1, keepdims=True) + epsilon)
    return (as_float * inverse * gain).astype(jnp.bfloat16)


def inverse_of(migration):
    slot_ids = jnp.arange(migration.shape[0], dtype=jnp.int32)
    return jnp.sum(jnp.where(migration[None, :] == slot_ids[:, None], slot_ids[None, :], 0), axis=1)


def per_device(
    step_inputs,
    attention_gain,
    query_weight,
    key_value_weight,
    output_weight,
    prompt_cache,
    page_table,
    cache_lengths,
    migration,
    parents,
    routes,
    feedforward_gain,
    router_weight,
    expert_gate,
    expert_up,
    expert_down,
    shared_gate,
    shared_up,
    shared_down,
):
    n_req = lax.axis_size("req")
    n_blk = lax.axis_size("blk")
    req_index = lax.axis_index("req")
    blk_index = lax.axis_index("blk")
    steps, rows_dev, width_local = step_inputs.shape
    rows = steps * rows_dev
    _, pages_local, page_length, features = prompt_cache.shape
    model_width = width_local * n_blk
    slices_dev = expert_gate.shape[0]
    hidden_dev = expert_gate.shape[2]
    split_count = FFE // hidden_dev
    inverse = inverse_of(migration)

    here = step_inputs.reshape(rows, width_local)
    x_local = permute_rows(here, migration, (0, 1))
    all_parents = lax.all_gather(parents, "req")
    all_routes = lax.all_gather(routes, "req")
    my_parents = lax.dynamic_index_in_dim(all_parents, migration[req_index], 0, False)
    x = gather_columns(x_local, "blk", 2)
    normed_x = norm_rows(x, attention_gain)
    q_local = jnp.dot(normed_x, query_weight, preferred_element_type=jnp.float32)
    kv_local = jnp.dot(normed_x, key_value_weight, preferred_element_type=jnp.float32)
    q_blocks, kv_blocks = push(
        [q_local.astype(jnp.bfloat16), kv_local.astype(jnp.bfloat16)], "blk", 3, gather=True
    )
    q = jnp.transpose(q_blocks, (1, 0, 2)).reshape(rows, -1)
    kv = jnp.transpose(kv_blocks, (1, 0, 2)).reshape(rows, -1)

    length = cache_lengths[req_index]
    half = HEAD_WIDTH // 2
    frequency = rope_base ** (-2.0 * jnp.arange(half, dtype=jnp.float32) / HEAD_WIDTH)
    positions = length + jnp.arange(rows, dtype=jnp.int32) // rows_dev
    angles = positions.astype(jnp.float32)[:, None] * frequency
    cosines, sines = jnp.cos(angles), jnp.sin(angles)
    cosines = jnp.concatenate([cosines, cosines], axis=1)
    sines = jnp.concatenate([-sines, sines], axis=1)
    row_ids = jnp.arange(rows, dtype=jnp.int32)
    parent_rows = jnp.concatenate(
        [
            jnp.full((rows_dev,), -1, jnp.int32),
            jnp.arange(rows_dev, dtype=jnp.int32) // BEAMS * BEAMS + my_parents[0],
        ]
    )
    parent = (parent_rows[:, None] == row_ids[None, :]).astype(jnp.bfloat16)
    table = lax.dynamic_index_in_dim(page_table, req_index, 0, False)[0]
    local_ids = jnp.arange(pages_local, dtype=jnp.int32)
    logical = jnp.sum(jnp.where(table[None, :] == local_ids[:, None], local_ids[None, :], 0), axis=1)
    key_positions = (
        (logical * n_blk + blk_index)[:, None] * page_length
        + jnp.arange(page_length, dtype=jnp.int32)[None, :]
    ).reshape(1, -1)
    tail = jnp.stack([(blk_index == 0).astype(jnp.int32), length])
    part, lse = attention_part(
        tail,
        q,
        kv,
        parent,
        cosines,
        sines,
        key_positions,
        prompt_cache.reshape(pages_local * page_length, features),
    )
    share = rows // n_blk
    parts, lses = push(
        [part.reshape(n_blk, share, -1), lse.reshape(n_blk, share, HEAD_WIDTH)], "blk", 4
    )
    heads_mine = merge(parts, lses)
    (heads,) = push([heads_mine], "blk", 5, gather=True)
    heads = heads.reshape(rows, -1)
    attended_there = (
        x_local.astype(jnp.float32)
        + jnp.dot(heads, output_weight, preferred_element_type=jnp.float32)
    ).astype(jnp.bfloat16)
    attended_local = permute_rows(attended_there, inverse, (6, 7))
    attended = gather_columns(attended_local, "blk", 8)
    normed_h = norm_rows(attended, feedforward_gain)

    slice_ids = (
        jnp.arange(n_req, dtype=jnp.int32)[:, None] * n_blk + blk_index
    ) * slices_dev + jnp.arange(slices_dev, dtype=jnp.int32)[None, :]
    targets = slice_ids // split_count
    chosen = routes.reshape(rows, TOPK)
    named = jnp.any(chosen[:, :, None] == jnp.arange(E, dtype=jnp.int32), axis=1)
    logits = jnp.dot(normed_h, router_weight, preferred_element_type=jnp.float32)
    raised = jnp.where(named, jnp.exp(jnp.where(named, logits, 0.0)), 0.0)
    gates = raised / jnp.sum(raised, axis=1, keepdims=True)
    match = jnp.any(chosen[None, None] == targets[:, :, None, None], axis=-1)
    places = jnp.cumsum(
        match.reshape(n_req, slices_dev * rows).astype(jnp.int32), axis=1
    ).reshape(match.shape)
    places = jnp.where(match, places - 1, -1)
    my_targets = targets[req_index]
    arriving = jnp.sum(
        jnp.any(
            all_routes.reshape(n_req, rows, TOPK)[:, None]
            == my_targets[None, :, None, None],
            axis=-1,
        ).astype(jnp.int32),
        axis=2,
    )
    ends = jnp.cumsum(arriving, axis=1)
    starts = ends - arriving
    expert_of = (targets[:, :, None] == jnp.arange(E, dtype=jnp.int32)).astype(jnp.float32)
    gate_of = jnp.einsum(
        "rje,ie->rji", expert_of, gates, precision=lax.Precision.HIGHEST
    )

    def experts(room):
        slots = jnp.arange(room, dtype=jnp.int32)
        taken = places[:, None] == slots[None, :, None, None]
        dispatch = jnp.any(taken, axis=2).reshape(n_req * room, rows).astype(jnp.bfloat16)
        mixing = jnp.sum(jnp.where(taken, gate_of[:, None], 0.0), axis=2).reshape(
            n_req * room, rows
        )
        sending = (
            jnp.dot(dispatch, normed_h, preferred_element_type=jnp.float32)
            .astype(jnp.bfloat16)
            .reshape(n_req, room, model_width)
        )
        (arrived,) = push([sending], "req", 9)
        members = arrived.reshape(n_req * room, model_width)
        mine = (
            (slots[None, :, None] >= starts[:, None]) & (slots[None, :, None] < ends[:, None])
        ).reshape(n_req * room, slices_dev)
        produced = jnp.zeros((n_req * room, model_width), jnp.float32)
        for j in range(slices_dev):
            gate_part = jnp.dot(members, expert_gate[j], preferred_element_type=jnp.float32)
            up_part = jnp.dot(members, expert_up[j], preferred_element_type=jnp.float32)
            hidden = jnp.where(
                mine[:, j : j + 1], jax.nn.silu(gate_part) * up_part, 0.0
            ).astype(jnp.bfloat16)
            produced += jnp.dot(hidden, expert_down[j], preferred_element_type=jnp.float32)
        (returned,) = push(
            [produced.astype(jnp.bfloat16).reshape(n_req, room, model_width)], "req", 10
        )
        returned = returned.reshape(n_req * room, model_width)
        high = mixing.astype(jnp.bfloat16)
        low = (mixing - high.astype(jnp.float32)).astype(jnp.bfloat16)
        return jnp.dot(high.T, returned, preferred_element_type=jnp.float32) + jnp.dot(
            low.T, returned, preferred_element_type=jnp.float32
        )

    routed = experts(slices_dev * steps * CAP)
    shared_act = (
        jax.nn.silu(jnp.dot(normed_h, shared_gate, preferred_element_type=jnp.float32))
        * jnp.dot(normed_h, shared_up, preferred_element_type=jnp.float32)
    ).astype(jnp.bfloat16)
    terms = routed + jnp.dot(shared_act, shared_down, preferred_element_type=jnp.float32)
    blocks = jnp.transpose(
        terms.astype(jnp.bfloat16).reshape(rows, n_blk, width_local), (1, 0, 2)
    )
    (blocks,) = push([blocks], "blk", 11)
    summed = jnp.sum(blocks.astype(jnp.float32), axis=0)
    out = (attended_local.astype(jnp.float32) + summed).astype(jnp.bfloat16)
    return out.reshape(steps, rows_dev, width_local)


def solution(mesh):
    in_specs = (
        P(None, "req", "blk"),
        P(),
        P(None, "blk"),
        P(None, "blk"),
        P(None, "blk"),
        P("req", "blk", None, None),
        P(None, "blk", None),
        P(),
        P(),
        P(None, "req"),
        P(None, "req", None),
        P(),
        P(),
        P(("req", "blk"), None, None),
        P(("req", "blk"), None, None),
        P(("req", "blk"), None, None),
        P(None, "blk"),
        P(None, "blk"),
        P("blk", None),
    )
    out_specs = P(None, "req", "blk")
    return jax.shard_map(
        per_device, mesh=mesh, in_specs=in_specs, out_specs=out_specs, check_vma=False
    )
```

```python
import functools

import jax
import jax.numpy as jnp
from jax import lax
from jax.experimental import pallas as pl
from jax.experimental.pallas import tpu as pltpu
from jax.sharding import PartitionSpec as P

QUERY_HEADS = 20
KEY_VALUE_HEADS = 4
HEAD_WIDTH = 128
E = 64
FFE = 1536
TOPK = 6
BEAMS = 8
CAP = 16
GROUP = QUERY_HEADS // KEY_VALUE_HEADS

epsilon = 1e-05
rope_base = 500000.0
masked_floor = -1e30
MIB = 1 << 20


def push_kernel(axis, n, count, gather, *refs):
    ins, outs = refs[:count], refs[count : 2 * count]
    send_sem, recv_sem, local_sem = refs[2 * count :]
    me = lax.axis_index(axis)
    barrier = pltpu.get_barrier_semaphore()
    for k in range(1, n):
        pl.semaphore_signal(
            barrier,
            inc=1,
            device_id={axis: lax.rem(me + k, n)},
            device_id_type=pl.DeviceIdType.MESH,
        )
    pl.semaphore_wait(barrier, n - 1)
    copies = []
    for k in range(1, n):
        to = lax.rem(me + k, n)
        for i in range(count):
            copy = pltpu.make_async_remote_copy(
                src_ref=ins[i] if gather[i] else ins[i].at[to],
                dst_ref=outs[i].at[me],
                send_sem=send_sem.at[i, k],
                recv_sem=recv_sem.at[i, k],
                device_id={axis: to},
                device_id_type=pl.DeviceIdType.MESH,
            )
            copy.start()
            copies.append(copy)
    own = []
    for i in range(count):
        copy = pltpu.make_async_copy(
            ins[i] if gather[i] else ins[i].at[me], outs[i].at[me], local_sem.at[i]
        )
        copy.start()
        own.append(copy)
    for copy in own:
        copy.wait()
    for copy in copies:
        copy.wait()


def push(arrays, axis, collective_id, gather=False):
    n = lax.axis_size(axis)
    count = len(arrays)
    if not isinstance(gather, tuple):
        gather = (gather,) * count
    shapes = [
        jax.ShapeDtypeStruct(((n,) + a.shape) if whole else a.shape, a.dtype)
        for a, whole in zip(arrays, gather)
    ]
    return pl.pallas_call(
        functools.partial(push_kernel, axis, n, count, gather),
        out_shape=shapes,
        in_specs=[pl.BlockSpec(memory_space=pl.ANY)] * count,
        out_specs=[pl.BlockSpec(memory_space=pl.ANY)] * count,
        scratch_shapes=[
            pltpu.SemaphoreType.DMA((count, n)),
            pltpu.SemaphoreType.DMA((count, n)),
            pltpu.SemaphoreType.DMA((count,)),
        ],
        compiler_params=pltpu.CompilerParams(collective_id=collective_id, has_side_effects=True),
        name=f"push_{axis}_{collective_id}",
    )(*arrays)


def gather_columns(array, axis, collective_id):
    (blocks,) = push([array], axis, collective_id, gather=True)
    return jnp.transpose(blocks, (1, 0, 2)).reshape(array.shape[0], -1)


def permute_rows(rows, block_for, ids, beside=()):
    n = lax.axis_size("req")
    pieces = rows.reshape(n, rows.shape[0] // n, rows.shape[1])
    spread, *gathered = push(
        [pieces, *beside], "req", ids[0], gather=(False,) + (True,) * len(beside)
    )
    (arrived,) = push([jnp.take(spread, block_for, axis=0)], "req", ids[1])
    return (arrived.reshape(rows.shape), *gathered)


def experts_kernel(
    n, sending, gate_hbm, up_hbm, down_hbm, high_ref, low_ref, shared_ref, out_ref,
    gate, up, down, held, hidden, back, weight_sem, send_sem, recv_sem, home_sem, back_sem, own_sem,
):
    me = lax.axis_index("req")
    near = n // 2
    mine = lax.rem(me, near)
    base = me - mine
    other = lax.rem(base + near, n)

    def target(i):
        return (base if i < near else other) + lax.rem(mine + i % near, near)

    def source(i):
        return (base if i < near else other) + lax.rem(mine + near - i % near, near)

    slices, _, width = gate.shape
    room = held.shape[1] // slices
    weights = []
    for j in range(slices):
        for number, (hbm, vmem) in enumerate(((gate_hbm, gate), (up_hbm, up), (down_hbm, down))):
            copy = pltpu.make_async_copy(hbm.at[j], vmem.at[j], weight_sem.at[3 * j + number])
            copy.start()
            weights.append(copy)

    barrier = pltpu.get_barrier_semaphore()
    for k in range(1, n):
        pl.semaphore_signal(
            barrier,
            inc=1,
            device_id={"req": lax.rem(me + k, n)},
            device_id_type=pl.DeviceIdType.MESH,
        )
    pl.semaphore_wait(barrier, n - 1)

    there, home = {}, {}
    for i in list(range(near, n)) + list(range(1, near)):
        there[i] = pltpu.make_async_remote_copy(
            src_ref=sending.at[target(i)],
            dst_ref=held.at[i],
            send_sem=send_sem.at[i],
            recv_sem=recv_sem.at[i],
            device_id={"req": target(i)},
            device_id_type=pl.DeviceIdType.MESH,
        )
        there[i].start()
    own = pltpu.make_async_copy(sending.at[me], held.at[0], own_sem.at[0])
    own.start()

    tile = 256 if width % 256 == 0 else 128
    model = down.shape[2]
    wide = 512

    def chunk(first, last, wait_weights):
        count = last - first
        for i in range(first, last):
            if i == 0:
                own.wait()
            else:
                there[i].wait_recv()
        for j in range(slices):
            rows_at = pl.ds(j * room, room)
            if wait_weights:
                weights[3 * j].wait()
                weights[3 * j + 1].wait()

            @pl.loop(0, width // tile)
            def _(f):
                at = pl.ds(pl.multiple_of(f * tile, tile), tile)
                rows = held[first:last, rows_at, :].reshape(count * room, model)
                g = jnp.dot(rows, gate[j, :, at], preferred_element_type=jnp.float32)
                u = jnp.dot(rows, up[j, :, at], preferred_element_type=jnp.float32)
                hidden[: count * room, at] = (g / (1.0 + jnp.exp(-g)) * u).astype(jnp.bfloat16)

            if wait_weights:
                weights[3 * j + 2].wait()

            @pl.loop(0, model // wide)
            def _(c):
                at = pl.ds(pl.multiple_of(c * wide, wide), wide)
                produced = jnp.dot(
                    hidden[: count * room, :], down[j, :, at], preferred_element_type=jnp.float32
                )
                held[first:last, rows_at, at] = produced.astype(jnp.bfloat16).reshape(
                    count, room, wide
                )

        for i in range(first, last):
            if i == 0:
                continue
            home[i] = pltpu.make_async_remote_copy(
                src_ref=held.at[i],
                dst_ref=back.at[me],
                send_sem=home_sem.at[i],
                recv_sem=back_sem.at[i],
                device_id={"req": source(i)},
                device_id_type=pl.DeviceIdType.MESH,
            )
            home[i].start()

    chunk(0, near, True)
    own_back = pltpu.make_async_copy(held.at[0], back.at[me], own_sem.at[1])
    own_back.start()
    chunk(near, near + near // 2, False)
    chunk(near + near // 2, n, False)
    own_back.wait()
    for i in range(1, n):
        there[i].wait_send()
        home[i].wait()
    block = out_ref.shape[2]
    returned = back[...].reshape(-1, model)
    for b in range(out_ref.shape[0]):
        at = pl.ds(b * block, block)
        part = returned[:, b * block : (b + 1) * block]
        routed = jnp.dot(high_ref[...], part, preferred_element_type=jnp.float32) + jnp.dot(
            low_ref[...], part, preferred_element_type=jnp.float32
        )
        out_ref[b] = (routed + shared_ref[:, at]).astype(jnp.bfloat16)


def run_experts(sending, gate, up, down, high, low, shared, n_blk, collective_id):
    n, taken, model = sending.shape
    slices, _, width = gate.shape
    rows = shared.shape[0]
    anywhere = pl.BlockSpec(memory_space=pl.ANY)
    vmem = pl.BlockSpec(memory_space=pltpu.VMEM)
    return pl.pallas_call(
        functools.partial(experts_kernel, n),
        out_shape=jax.ShapeDtypeStruct((n_blk, rows, model // n_blk), jnp.bfloat16),
        in_specs=[anywhere] * 4 + [vmem] * 3,
        out_specs=vmem,
        scratch_shapes=[
            pltpu.VMEM(gate.shape, gate.dtype),
            pltpu.VMEM(up.shape, up.dtype),
            pltpu.VMEM(down.shape, down.dtype),
            pltpu.VMEM((n, taken, model), jnp.bfloat16),
            pltpu.VMEM((n // 2 * taken // slices, width), jnp.bfloat16),
            pltpu.VMEM((n, taken, model), jnp.bfloat16),
            pltpu.SemaphoreType.DMA((3 * slices,)),
            pltpu.SemaphoreType.DMA((n,)),
            pltpu.SemaphoreType.DMA((n,)),
            pltpu.SemaphoreType.DMA((n,)),
            pltpu.SemaphoreType.DMA((n,)),
            pltpu.SemaphoreType.DMA((2,)),
        ],
        compiler_params=pltpu.CompilerParams(
            collective_id=collective_id, has_side_effects=True, vmem_limit_bytes=60 * MIB
        ),
        name="experts",
    )(sending, gate, up, down, high, low, shared)


def attention_kernel(
    tail_ref, q_ref, kv_ref, parent_ref, cos_ref, sin_ref, pos_ref, cache_ref, o_ref, lse_ref
):
    rows = q_ref.shape[0]
    scaling = HEAD_WIDTH ** (-0.5)
    key_width = KEY_VALUE_HEADS * HEAD_WIDTH
    cosines, sines = cos_ref[...], sin_ref[...]

    def rotated(block):
        block = block.astype(jnp.float32)
        half = HEAD_WIDTH // 2
        swapped = jnp.concatenate([block[:, half:], block[:, :half]], axis=1)
        return (block * cosines + swapped * sines).astype(jnp.bfloat16)

    tails_here = tail_ref[0] > 0
    valid = pos_ref[...] < tail_ref[1]
    parent = parent_ref[...]
    has_parent = jnp.sum(parent.astype(jnp.float32), axis=1, keepdims=True) > 0.5
    lse_ref[...] = jnp.full(lse_ref.shape, masked_floor, jnp.float32)
    for kv_head in range(KEY_VALUE_HEADS):
        keys_at = pl.ds(kv_head * HEAD_WIDTH, HEAD_WIDTH)
        values_at = pl.ds(key_width + kv_head * HEAD_WIDTH, HEAD_WIDTH)
        own_key = rotated(kv_ref[:, keys_at])
        own_value = kv_ref[:, values_at]
        parent_key = jnp.dot(parent, own_key, preferred_element_type=jnp.float32)
        parent_value = jnp.dot(parent, own_value, preferred_element_type=jnp.float32)
        own_key = own_key.astype(jnp.float32)
        own_value = own_value.astype(jnp.float32)
        keys = cache_ref[:, keys_at]
        values = cache_ref[:, values_at]
        for g in range(GROUP):
            head = kv_head * GROUP + g
            at = pl.ds(head * HEAD_WIDTH, HEAD_WIDTH)
            query = rotated(q_ref[:, at])
            scores = (
                lax.dot_general(
                    query, keys, (((1,), (1,)), ((), ())), preferred_element_type=jnp.float32
                )
                * scaling
            )
            query = query.astype(jnp.float32)
            own = jnp.sum(query * own_key, axis=1, keepdims=True) * scaling
            par = jnp.sum(query * parent_key, axis=1, keepdims=True) * scaling
            own = jnp.where(tails_here, own, masked_floor)
            par = jnp.where(has_parent & tails_here, par, masked_floor)
            scores = jnp.where(valid, scores, masked_floor)
            peak = jnp.maximum(jnp.max(scores, axis=1, keepdims=True), jnp.maximum(own, par))
            probs = jnp.where(valid, jnp.exp(scores - peak), 0.0)
            own = jnp.where(tails_here, jnp.exp(own - peak), 0.0)
            par = jnp.where(has_parent & tails_here, jnp.exp(par - peak), 0.0)
            total = jnp.sum(probs, axis=1, keepdims=True) + own + par
            weighted = jnp.dot(
                probs.astype(jnp.bfloat16), values, preferred_element_type=jnp.float32
            )
            weighted += own.astype(jnp.bfloat16).astype(jnp.float32) * own_value
            weighted += par.astype(jnp.bfloat16).astype(jnp.float32) * parent_value
            live = total > 0.0
            safe = jnp.where(live, total, 1.0)
            o_ref[:, at] = (weighted / safe).astype(jnp.bfloat16)
            lse_ref[:, head : head + 1] = jnp.where(live, peak + jnp.log(safe), masked_floor)


def attention_part(tail, q, kv, parent, cosines, sines, positions, cache):
    rows = q.shape[0]
    vmem = pl.BlockSpec(memory_space=pltpu.VMEM)
    return pl.pallas_call(
        attention_kernel,
        out_shape=[
            jax.ShapeDtypeStruct(q.shape, jnp.bfloat16),
            jax.ShapeDtypeStruct((rows, HEAD_WIDTH), jnp.float32),
        ],
        in_specs=[pl.BlockSpec(memory_space=pltpu.SMEM)] + [vmem] * 7,
        out_specs=[vmem] * 2,
        compiler_params=pltpu.CompilerParams(vmem_limit_bytes=40 * MIB),
        name="attention_part",
    )(tail, q, kv, parent, cosines, sines, positions, cache)


def merge_kernel(o_ref, lse_ref, out_ref):
    n = o_ref.shape[0]
    peaks = lse_ref[0]
    for b in range(1, n):
        peaks = jnp.maximum(peaks, lse_ref[b])
    scales = [jnp.exp(lse_ref[b] - peaks) for b in range(n)]
    total = scales[0]
    for b in range(1, n):
        total = total + scales[b]
    scales = [scale / total for scale in scales]
    for head in range(QUERY_HEADS):
        at = pl.ds(head * HEAD_WIDTH, HEAD_WIDTH)
        acc = o_ref[0, :, at].astype(jnp.float32) * scales[0][:, head : head + 1]
        for b in range(1, n):
            acc += o_ref[b, :, at].astype(jnp.float32) * scales[b][:, head : head + 1]
        out_ref[:, at] = acc.astype(jnp.bfloat16)


def merge(parts, lse):
    vmem = pl.BlockSpec(memory_space=pltpu.VMEM)
    return pl.pallas_call(
        merge_kernel,
        out_shape=jax.ShapeDtypeStruct(parts.shape[1:], jnp.bfloat16),
        in_specs=[vmem] * 2,
        out_specs=vmem,
        compiler_params=pltpu.CompilerParams(vmem_limit_bytes=40 * MIB),
        name="merge",
    )(parts, lse)


def norm_rows(values, gain):
    as_float = values.astype(jnp.float32)
    inverse = lax.rsqrt(jnp.mean(as_float * as_float, axis=-1, keepdims=True) + epsilon)
    return (as_float * inverse * gain).astype(jnp.bfloat16)


def inverse_of(migration):
    slot_ids = jnp.arange(migration.shape[0], dtype=jnp.int32)
    return jnp.sum(jnp.where(migration[None, :] == slot_ids[:, None], slot_ids[None, :], 0), axis=1)


def per_device(
    step_inputs,
    attention_gain,
    query_weight,
    key_value_weight,
    output_weight,
    prompt_cache,
    page_table,
    cache_lengths,
    migration,
    parents,
    routes,
    feedforward_gain,
    router_weight,
    expert_gate,
    expert_up,
    expert_down,
    shared_gate,
    shared_up,
    shared_down,
):
    n_req = lax.axis_size("req")
    n_blk = lax.axis_size("blk")
    req_index = lax.axis_index("req")
    blk_index = lax.axis_index("blk")
    steps, rows_dev, width_local = step_inputs.shape
    rows = steps * rows_dev
    _, pages_local, page_length, features = prompt_cache.shape
    model_width = width_local * n_blk
    slices_dev = expert_gate.shape[0]
    hidden_dev = expert_gate.shape[2]
    split_count = FFE // hidden_dev
    inverse = inverse_of(migration)

    here = step_inputs.reshape(rows, width_local)
    padded = jnp.pad(parents, ((0, 0), (0, -parents.shape[1] % HEAD_WIDTH)))
    x_local, all_parents = permute_rows(here, migration, (0, 1), (padded,))
    my_parents = lax.dynamic_index_in_dim(all_parents, migration[req_index], 0, False)[
        :, : parents.shape[1]
    ]
    x = gather_columns(x_local, "blk", 2)
    normed_x = norm_rows(x, attention_gain)
    q_local = jnp.dot(normed_x, query_weight, preferred_element_type=jnp.float32)
    kv_local = jnp.dot(normed_x, key_value_weight, preferred_element_type=jnp.float32)
    q_blocks, kv_blocks = push(
        [q_local.astype(jnp.bfloat16), kv_local.astype(jnp.bfloat16)], "blk", 3, gather=True
    )
    q = jnp.transpose(q_blocks, (1, 0, 2)).reshape(rows, -1)
    kv = jnp.transpose(kv_blocks, (1, 0, 2)).reshape(rows, -1)

    length = cache_lengths[req_index]
    half = HEAD_WIDTH // 2
    frequency = rope_base ** (-2.0 * jnp.arange(half, dtype=jnp.float32) / HEAD_WIDTH)
    positions = length + jnp.arange(rows, dtype=jnp.int32) // rows_dev
    angles = positions.astype(jnp.float32)[:, None] * frequency
    cosines, sines = jnp.cos(angles), jnp.sin(angles)
    cosines = jnp.concatenate([cosines, cosines], axis=1)
    sines = jnp.concatenate([-sines, sines], axis=1)
    row_ids = jnp.arange(rows, dtype=jnp.int32)
    parent_rows = jnp.concatenate(
        [
            jnp.full((rows_dev,), -1, jnp.int32),
            jnp.arange(rows_dev, dtype=jnp.int32) // BEAMS * BEAMS + my_parents[0],
        ]
    )
    parent = (parent_rows[:, None] == row_ids[None, :]).astype(jnp.bfloat16)
    table = lax.dynamic_index_in_dim(page_table, req_index, 0, False)[0]
    local_ids = jnp.arange(pages_local, dtype=jnp.int32)
    logical = jnp.sum(jnp.where(table[None, :] == local_ids[:, None], local_ids[None, :], 0), axis=1)
    key_positions = (
        (logical * n_blk + blk_index)[:, None] * page_length
        + jnp.arange(page_length, dtype=jnp.int32)[None, :]
    ).reshape(1, -1)
    tail = jnp.stack([(blk_index == 0).astype(jnp.int32), length])
    part, lse = attention_part(
        tail,
        q,
        kv,
        parent,
        cosines,
        sines,
        key_positions,
        prompt_cache.reshape(pages_local * page_length, features),
    )
    share = rows // n_blk
    parts, lses = push(
        [part.reshape(n_blk, share, -1), lse.reshape(n_blk, share, HEAD_WIDTH)], "blk", 4
    )
    heads_mine = merge(parts, lses)
    (heads,) = push([heads_mine], "blk", 5, gather=True)
    heads = heads.reshape(rows, -1)
    attended_there = (
        x_local.astype(jnp.float32)
        + jnp.dot(heads, output_weight, preferred_element_type=jnp.float32)
    ).astype(jnp.bfloat16)
    (attended_local,) = permute_rows(attended_there, inverse, (6, 7))
    attended = gather_columns(attended_local, "blk", 8)
    normed_h = norm_rows(attended, feedforward_gain)

    room = steps * CAP
    slice_ids = (
        jnp.arange(n_req, dtype=jnp.int32)[:, None] * n_blk + blk_index
    ) * slices_dev + jnp.arange(slices_dev, dtype=jnp.int32)[None, :]
    targets = (slice_ids // split_count).reshape(-1)
    chosen = routes.reshape(rows, TOPK)
    named = jnp.any(chosen[:, :, None] == jnp.arange(E, dtype=jnp.int32), axis=1)
    match = jnp.any(chosen[None] == targets[:, None, None], axis=-1)
    below = (row_ids[:, None] <= row_ids[None, :]).astype(jnp.bfloat16)
    places = jnp.dot(
        match.astype(jnp.bfloat16), below, preferred_element_type=jnp.float32
    ).astype(jnp.int32)
    places = jnp.where(match, places - 1, -1)
    taken = places[:, None, :] == jnp.arange(room, dtype=jnp.int32)[None, :, None]
    dispatch = taken.reshape(-1, rows)
    sending = (
        jnp.dot(dispatch.astype(jnp.bfloat16), normed_h, preferred_element_type=jnp.float32)
        .astype(jnp.bfloat16)
        .reshape(n_req, slices_dev * room, model_width)
    )
    logits = jnp.dot(normed_h, router_weight, preferred_element_type=jnp.float32)
    raised = jnp.where(named, jnp.exp(jnp.where(named, logits, 0.0)), 0.0)
    gates = raised / jnp.sum(raised, axis=1, keepdims=True)
    expert_of = (targets[:, None] == jnp.arange(E, dtype=jnp.int32)).astype(jnp.float32)
    gate_of = jnp.dot(gates, expert_of.T, precision=lax.Precision.HIGHEST)
    mixing = jnp.where(
        jnp.transpose(taken, (2, 0, 1)), gate_of[:, :, None], 0.0
    ).reshape(rows, -1)
    high = mixing.astype(jnp.bfloat16)
    low = (mixing - high.astype(jnp.float32)).astype(jnp.bfloat16)
    shared_act = (
        jax.nn.silu(jnp.dot(normed_h, shared_gate, preferred_element_type=jnp.float32))
        * jnp.dot(normed_h, shared_up, preferred_element_type=jnp.float32)
    ).astype(jnp.bfloat16)
    shared = jnp.dot(shared_act, shared_down, preferred_element_type=jnp.float32)
    blocks = run_experts(
        sending, expert_gate, expert_up, expert_down, high, low, shared, n_blk, 9
    )
    (blocks,) = push([blocks], "blk", 11)
    summed = jnp.sum(blocks.astype(jnp.float32), axis=0)
    out = (attended_local.astype(jnp.float32) + summed).astype(jnp.bfloat16)
    return out.reshape(steps, rows_dev, width_local)


def solution(mesh):
    in_specs = (
        P(None, "req", "blk"),
        P(),
        P(None, "blk"),
        P(None, "blk"),
        P(None, "blk"),
        P("req", "blk", None, None),
        P(None, "blk", None),
        P(),
        P(),
        P(None, "req"),
        P(None, "req", None),
        P(),
        P(),
        P(("req", "blk"), None, None),
        P(("req", "blk"), None, None),
        P(("req", "blk"), None, None),
        P(None, "blk"),
        P(None, "blk"),
        P("blk", None),
    )
    out_specs = P(None, "req", "blk")
    return jax.shard_map(
        per_device, mesh=mesh, in_specs=in_specs, out_specs=out_specs, check_vma=False
    )
```

```python
import functools

import jax
import jax.numpy as jnp
from jax import lax
from jax.experimental import pallas as pl
from jax.experimental.pallas import tpu as pltpu
from jax.sharding import PartitionSpec as P

QUERY_HEADS = 20
KEY_VALUE_HEADS = 4
HEAD_WIDTH = 128
E = 64
FFE = 1536
TOPK = 6
BEAMS = 8
CAP = 16
GROUP = QUERY_HEADS // KEY_VALUE_HEADS

epsilon = 1e-05
rope_base = 500000.0
masked_floor = -1e30
MIB = 1 << 20


def push_kernel(axis, n, count, gather, *refs):
    ins, outs = refs[:count], refs[count : 2 * count]
    send_sem, recv_sem, local_sem = refs[2 * count :]
    me = lax.axis_index(axis)
    barrier = pltpu.get_barrier_semaphore()
    for k in range(1, n):
        pl.semaphore_signal(
            barrier,
            inc=1,
            device_id={axis: lax.rem(me + k, n)},
            device_id_type=pl.DeviceIdType.MESH,
        )
    pl.semaphore_wait(barrier, n - 1)
    copies = []
    for k in range(1, n):
        to = lax.rem(me + k, n)
        for i in range(count):
            copy = pltpu.make_async_remote_copy(
                src_ref=ins[i] if gather[i] else ins[i].at[to],
                dst_ref=outs[i].at[me],
                send_sem=send_sem.at[i, k],
                recv_sem=recv_sem.at[i, k],
                device_id={axis: to},
                device_id_type=pl.DeviceIdType.MESH,
            )
            copy.start()
            copies.append(copy)
    own = []
    for i in range(count):
        copy = pltpu.make_async_copy(
            ins[i] if gather[i] else ins[i].at[me], outs[i].at[me], local_sem.at[i]
        )
        copy.start()
        own.append(copy)
    for copy in own:
        copy.wait()
    for copy in copies:
        copy.wait()


def push(arrays, axis, collective_id, gather=False):
    n = lax.axis_size(axis)
    count = len(arrays)
    if not isinstance(gather, tuple):
        gather = (gather,) * count
    shapes = [
        jax.ShapeDtypeStruct(((n,) + a.shape) if whole else a.shape, a.dtype)
        for a, whole in zip(arrays, gather)
    ]
    return pl.pallas_call(
        functools.partial(push_kernel, axis, n, count, gather),
        out_shape=shapes,
        in_specs=[pl.BlockSpec(memory_space=pl.ANY)] * count,
        out_specs=[pl.BlockSpec(memory_space=pl.ANY)] * count,
        scratch_shapes=[
            pltpu.SemaphoreType.DMA((count, n)),
            pltpu.SemaphoreType.DMA((count, n)),
            pltpu.SemaphoreType.DMA((count,)),
        ],
        compiler_params=pltpu.CompilerParams(collective_id=collective_id, has_side_effects=True),
        name=f"push_{axis}_{collective_id}",
    )(*arrays)


def route_kernel(n, n_blk, extra, block_for, gain_ref, pieces, *refs):
    besides, refs = refs[:extra], refs[extra:]
    normed_ref, rows_ref, *refs = refs
    gathered, refs = refs[:extra], refs[extra:]
    spread, staged, landed, wide, hop_send, hop_recv, local_sem = refs
    me, blk = lax.axis_index("req"), lax.axis_index("blk")
    barrier = pltpu.get_barrier_semaphore()

    def at(axis, k):
        here, size = (me, n) if axis == "req" else (blk, n_blk)
        return {axis: lax.rem(here + k, size)}

    partners = [("req", k) for k in range(1, n)] + [("blk", k) for k in range(1, n_blk)]
    for axis, k in partners:
        pl.semaphore_signal(
            barrier, inc=1, device_id=at(axis, k), device_id_type=pl.DeviceIdType.MESH
        )
    pl.semaphore_wait(barrier, len(partners))

    def send(source, landing, phase, axis, k):
        copy = pltpu.make_async_remote_copy(
            src_ref=source,
            dst_ref=landing,
            send_sem=hop_send.at[phase, k],
            recv_sem=hop_recv.at[phase, k],
            device_id=at(axis, k),
            device_id_type=pl.DeviceIdType.MESH,
        )
        copy.start()
        return copy

    def keep(source, landing, number):
        copy = pltpu.make_async_copy(source, landing, local_sem.at[number])
        copy.start()
        return copy

    copies = [
        send(pieces.at[lax.rem(me + k, n)], spread.at[me], 0, "req", k) for k in range(1, n)
    ]
    copies.append(keep(pieces.at[me], spread.at[me], 0))
    late = []
    for i in range(extra):
        late += [send(besides[i], gathered[i].at[me], 3 + i, "req", k) for k in range(1, n)]
        late.append(keep(besides[i], gathered[i].at[me], 3 + i))
    for copy in copies:
        copy.wait()
    for d in range(n):
        staged[d] = spread[block_for[d]]
    copies = [
        send(staged.at[lax.rem(me + k, n)], landed.at[me], 1, "req", k) for k in range(1, n)
    ]
    copies.append(keep(staged.at[me], landed.at[me], 1))
    for copy in copies:
        copy.wait()
    copies = [send(landed, wide.at[blk], 2, "blk", k) for k in range(1, n_blk)]
    copies.append(keep(landed, wide.at[blk], 2))
    rows_ref[...] = landed[...]
    for copy in copies + late:
        copy.wait()
    rows, model = normed_ref.shape
    width = model // n_blk
    blocks = [wide[b].astype(jnp.float32).reshape(rows, width) for b in range(n_blk)]
    squares = jnp.sum(blocks[0] * blocks[0], axis=1, keepdims=True)
    for block in blocks[1:]:
        squares += jnp.sum(block * block, axis=1, keepdims=True)
    inverse = lax.rsqrt(squares / model + epsilon)
    for b in range(n_blk):
        columns = slice(b * width, (b + 1) * width)
        normed_ref[:, columns] = (blocks[b] * inverse * gain_ref[:, columns]).astype(jnp.bfloat16)


def route_rows(rows, block_for, gain, collective_id, beside=()):
    n, n_blk = lax.axis_size("req"), lax.axis_size("blk")
    count, width = rows.shape
    extra = len(beside)
    pieces = rows.reshape(n, count // n, width)
    anywhere = pl.BlockSpec(memory_space=pl.ANY)
    vmem = pl.BlockSpec(memory_space=pltpu.VMEM)
    phases = 3 + extra
    hops = max(n, n_blk)
    normed, arrived, *gathered = pl.pallas_call(
        functools.partial(route_kernel, n, n_blk, extra),
        out_shape=[
            jax.ShapeDtypeStruct((count, width * n_blk), jnp.bfloat16),
            jax.ShapeDtypeStruct(pieces.shape, rows.dtype),
        ]
        + [jax.ShapeDtypeStruct((n,) + a.shape, a.dtype) for a in beside],
        in_specs=[pl.BlockSpec(memory_space=pltpu.SMEM), vmem, vmem] + [anywhere] * extra,
        out_specs=[vmem] * 2 + [anywhere] * extra,
        scratch_shapes=[pltpu.VMEM(pieces.shape, rows.dtype)] * 3
        + [
            pltpu.VMEM((n_blk,) + pieces.shape, rows.dtype),
            pltpu.SemaphoreType.DMA((phases, hops)),
            pltpu.SemaphoreType.DMA((phases, hops)),
            pltpu.SemaphoreType.DMA((phases,)),
        ],
        compiler_params=pltpu.CompilerParams(
            collective_id=collective_id, has_side_effects=True, vmem_limit_bytes=32 * MIB
        ),
        name=f"route_{collective_id}",
    )(block_for, gain.reshape(1, -1), pieces, *beside)
    return (normed, arrived.reshape(rows.shape), *gathered)


def experts_kernel(
    n, sending, gate_hbm, up_hbm, down_hbm, shared_gate, shared_up, shared_down,
    high_ref, low_ref, normed_ref, out_ref,
    gate, up, down, held, hidden, back, shared_act, shared_ref,
    weight_sem, send_sem, recv_sem, home_sem, back_sem, own_sem, *apart,
):
    me = lax.axis_index("req")
    near = n // 2
    mine = lax.rem(me, near)
    base = me - mine
    other = lax.rem(base + near, n)

    def target(i):
        return (base if i < near else other) + lax.rem(mine + i % near, near)

    def source(i):
        return (base if i < near else other) + lax.rem(mine + near - i % near, near)

    slices, _, width = gate.shape
    room = held.shape[1] // slices
    last = slices - 1
    shared_width = shared_gate.shape[1]
    if apart:
        places = apart
    else:
        columns = pl.ds(0, shared_width)
        places = (gate.at[last, :, columns], up.at[last, :, columns], down.at[last, columns, :])
    shared_copies = [
        pltpu.make_async_copy(hbm, vmem, weight_sem.at[3 * slices + number])
        for number, (hbm, vmem) in enumerate(zip((shared_gate, shared_up, shared_down), places))
    ]
    weights = [
        pltpu.make_async_copy(hbm.at[j], vmem.at[j], weight_sem.at[3 * j + number])
        for j in range(slices)
        for number, (hbm, vmem) in enumerate(((gate_hbm, gate), (up_hbm, up), (down_hbm, down)))
    ]
    for copy in shared_copies + weights[: 3 * last]:
        copy.start()

    barrier = pltpu.get_barrier_semaphore()
    for k in range(1, n):
        pl.semaphore_signal(
            barrier,
            inc=1,
            device_id={"req": lax.rem(me + k, n)},
            device_id_type=pl.DeviceIdType.MESH,
        )
    pl.semaphore_wait(barrier, n - 1)

    there, home = {}, {}
    for i in list(range(near, n)) + list(range(1, near)):
        there[i] = pltpu.make_async_remote_copy(
            src_ref=sending.at[target(i)],
            dst_ref=held.at[i],
            send_sem=send_sem.at[i],
            recv_sem=recv_sem.at[i],
            device_id={"req": target(i)},
            device_id_type=pl.DeviceIdType.MESH,
        )
        there[i].start()
    own = pltpu.make_async_copy(sending.at[me], held.at[0], own_sem.at[0])
    own.start()

    tile = 256 if width % 256 == 0 else 128
    model = down.shape[2]
    wide = 512

    for copy in shared_copies:
        copy.wait()
    step = 256 if shared_width % 256 == 0 else shared_width
    for f in range(0, shared_width, step):
        at = slice(f, f + step)
        g = jnp.dot(normed_ref[...], places[0][:, at], preferred_element_type=jnp.float32)
        u = jnp.dot(normed_ref[...], places[1][:, at], preferred_element_type=jnp.float32)
        shared_act[:, at] = (g / (1.0 + jnp.exp(-g)) * u).astype(jnp.bfloat16)
    for c in range(0, model, wide):
        at = slice(c, c + wide)
        shared_ref[:, at] = jnp.dot(
            shared_act[...], places[2][:, at], preferred_element_type=jnp.float32
        )
    for copy in weights[3 * last :]:
        copy.start()

    def chunk(first, last, wait_weights):
        count = last - first
        for i in range(first, last):
            if i == 0:
                own.wait()
            else:
                there[i].wait_recv()
        for j in range(slices):
            rows_at = pl.ds(j * room, room)
            if wait_weights:
                weights[3 * j].wait()
                weights[3 * j + 1].wait()

            @pl.loop(0, width // tile)
            def _(f):
                at = pl.ds(pl.multiple_of(f * tile, tile), tile)
                rows = held[first:last, rows_at, :].reshape(count * room, model)
                g = jnp.dot(rows, gate[j, :, at], preferred_element_type=jnp.float32)
                u = jnp.dot(rows, up[j, :, at], preferred_element_type=jnp.float32)
                hidden[: count * room, at] = (g / (1.0 + jnp.exp(-g)) * u).astype(jnp.bfloat16)

            if wait_weights:
                weights[3 * j + 2].wait()

            @pl.loop(0, model // wide)
            def _(c):
                at = pl.ds(pl.multiple_of(c * wide, wide), wide)
                produced = jnp.dot(
                    hidden[: count * room, :], down[j, :, at], preferred_element_type=jnp.float32
                )
                held[first:last, rows_at, at] = produced.astype(jnp.bfloat16).reshape(
                    count, room, wide
                )

        for i in range(first, last):
            if i == 0:
                continue
            home[i] = pltpu.make_async_remote_copy(
                src_ref=held.at[i],
                dst_ref=back.at[me],
                send_sem=home_sem.at[i],
                recv_sem=back_sem.at[i],
                device_id={"req": source(i)},
                device_id_type=pl.DeviceIdType.MESH,
            )
            home[i].start()

    chunk(0, near, True)
    own_back = pltpu.make_async_copy(held.at[0], back.at[me], own_sem.at[1])
    own_back.start()
    chunk(near, near + near // 2, False)
    chunk(near + near // 2, n, False)
    own_back.wait()
    for i in range(1, n):
        there[i].wait_send()
        home[i].wait()
    block = out_ref.shape[2]
    returned = back[...].reshape(-1, model)
    for b in range(out_ref.shape[0]):
        at = pl.ds(b * block, block)
        part = returned[:, b * block : (b + 1) * block]
        routed = jnp.dot(high_ref[...], part, preferred_element_type=jnp.float32) + jnp.dot(
            low_ref[...], part, preferred_element_type=jnp.float32
        )
        out_ref[b] = (routed + shared_ref[:, at]).astype(jnp.bfloat16)


def run_experts(sending, experts, shared, high, low, normed, n_blk, collective_id):
    n, taken, model = sending.shape
    gate, up, down = experts
    slices, _, width = gate.shape
    rows = normed.shape[0]
    shared_width = shared[0].shape[1]
    fits = shared_width % HEAD_WIDTH == 0 and shared_width <= width
    apart = [] if fits else [pltpu.VMEM(a.shape, a.dtype) for a in shared]
    anywhere = pl.BlockSpec(memory_space=pl.ANY)
    vmem = pl.BlockSpec(memory_space=pltpu.VMEM)
    return pl.pallas_call(
        functools.partial(experts_kernel, n),
        out_shape=jax.ShapeDtypeStruct((n_blk, rows, model // n_blk), jnp.bfloat16),
        in_specs=[anywhere] * 7 + [vmem] * 3,
        out_specs=vmem,
        scratch_shapes=[
            pltpu.VMEM(gate.shape, gate.dtype),
            pltpu.VMEM(up.shape, up.dtype),
            pltpu.VMEM(down.shape, down.dtype),
            pltpu.VMEM((n, taken, model), jnp.bfloat16),
            pltpu.VMEM((n // 2 * taken // slices, width), jnp.bfloat16),
            pltpu.VMEM((n, taken, model), jnp.bfloat16),
            pltpu.VMEM((rows, shared_width), jnp.bfloat16),
            pltpu.VMEM((rows, model), jnp.float32),
            pltpu.SemaphoreType.DMA((3 * slices + 3,)),
            pltpu.SemaphoreType.DMA((n,)),
            pltpu.SemaphoreType.DMA((n,)),
            pltpu.SemaphoreType.DMA((n,)),
            pltpu.SemaphoreType.DMA((n,)),
            pltpu.SemaphoreType.DMA((2,)),
            *apart,
        ],
        compiler_params=pltpu.CompilerParams(
            collective_id=collective_id, has_side_effects=True, vmem_limit_bytes=60 * MIB
        ),
        name="experts",
    )(sending, *experts, *shared, high, low, normed)


def attention_kernel(
    tail_ref, q_ref, kv_ref, parent_ref, cos_ref, sin_ref, pos_ref, cache_ref, o_ref, lse_ref
):
    rows = q_ref.shape[0]
    scaling = HEAD_WIDTH ** (-0.5)
    key_width = KEY_VALUE_HEADS * HEAD_WIDTH
    cosines, sines = cos_ref[...], sin_ref[...]

    def rotated(block):
        block = block.astype(jnp.float32)
        half = HEAD_WIDTH // 2
        swapped = jnp.concatenate([block[:, half:], block[:, :half]], axis=1)
        return (block * cosines + swapped * sines).astype(jnp.bfloat16)

    tails_here = tail_ref[0] > 0
    valid = pos_ref[...] < tail_ref[1]
    parent = parent_ref[...]
    has_parent = jnp.sum(parent.astype(jnp.float32), axis=1, keepdims=True) > 0.5
    lse_ref[...] = jnp.full(lse_ref.shape, masked_floor, jnp.float32)
    for kv_head in range(KEY_VALUE_HEADS):
        keys_at = pl.ds(kv_head * HEAD_WIDTH, HEAD_WIDTH)
        values_at = pl.ds(key_width + kv_head * HEAD_WIDTH, HEAD_WIDTH)
        own_key = rotated(kv_ref[:, keys_at])
        own_value = kv_ref[:, values_at]
        parent_key = jnp.dot(parent, own_key, preferred_element_type=jnp.float32)
        parent_value = jnp.dot(parent, own_value, preferred_element_type=jnp.float32)
        own_key = own_key.astype(jnp.float32)
        own_value = own_value.astype(jnp.float32)
        keys = cache_ref[:, keys_at]
        values = cache_ref[:, values_at]
        for g in range(GROUP):
            head = kv_head * GROUP + g
            at = pl.ds(head * HEAD_WIDTH, HEAD_WIDTH)
            query = rotated(q_ref[:, at])
            scores = (
                lax.dot_general(
                    query, keys, (((1,), (1,)), ((), ())), preferred_element_type=jnp.float32
                )
                * scaling
            )
            query = query.astype(jnp.float32)
            own = jnp.sum(query * own_key, axis=1, keepdims=True) * scaling
            par = jnp.sum(query * parent_key, axis=1, keepdims=True) * scaling
            own = jnp.where(tails_here, own, masked_floor)
            par = jnp.where(has_parent & tails_here, par, masked_floor)
            scores = jnp.where(valid, scores, masked_floor)
            peak = jnp.maximum(jnp.max(scores, axis=1, keepdims=True), jnp.maximum(own, par))
            probs = jnp.where(valid, jnp.exp(scores - peak), 0.0)
            own = jnp.where(tails_here, jnp.exp(own - peak), 0.0)
            par = jnp.where(has_parent & tails_here, jnp.exp(par - peak), 0.0)
            total = jnp.sum(probs, axis=1, keepdims=True) + own + par
            weighted = jnp.dot(
                probs.astype(jnp.bfloat16), values, preferred_element_type=jnp.float32
            )
            weighted += own.astype(jnp.bfloat16).astype(jnp.float32) * own_value
            weighted += par.astype(jnp.bfloat16).astype(jnp.float32) * parent_value
            live = total > 0.0
            safe = jnp.where(live, total, 1.0)
            o_ref[:, at] = (weighted / safe).astype(jnp.bfloat16)
            lse_ref[:, head : head + 1] = jnp.where(live, peak + jnp.log(safe), masked_floor)


def attention_part(tail, q, kv, parent, cosines, sines, positions, cache):
    rows = q.shape[0]
    vmem = pl.BlockSpec(memory_space=pltpu.VMEM)
    return pl.pallas_call(
        attention_kernel,
        out_shape=[
            jax.ShapeDtypeStruct(q.shape, jnp.bfloat16),
            jax.ShapeDtypeStruct((rows, HEAD_WIDTH), jnp.float32),
        ],
        in_specs=[pl.BlockSpec(memory_space=pltpu.SMEM)] + [vmem] * 7,
        out_specs=[vmem] * 2,
        compiler_params=pltpu.CompilerParams(vmem_limit_bytes=40 * MIB),
        name="attention_part",
    )(tail, q, kv, parent, cosines, sines, positions, cache)


def merge_kernel(o_ref, lse_ref, out_ref):
    n = o_ref.shape[0]
    peaks = lse_ref[0]
    for b in range(1, n):
        peaks = jnp.maximum(peaks, lse_ref[b])
    scales = [jnp.exp(lse_ref[b] - peaks) for b in range(n)]
    total = scales[0]
    for b in range(1, n):
        total = total + scales[b]
    scales = [scale / total for scale in scales]
    for head in range(QUERY_HEADS):
        at = pl.ds(head * HEAD_WIDTH, HEAD_WIDTH)
        acc = o_ref[0, :, at].astype(jnp.float32) * scales[0][:, head : head + 1]
        for b in range(1, n):
            acc += o_ref[b, :, at].astype(jnp.float32) * scales[b][:, head : head + 1]
        out_ref[:, at] = acc.astype(jnp.bfloat16)


def merge(parts, lse):
    vmem = pl.BlockSpec(memory_space=pltpu.VMEM)
    return pl.pallas_call(
        merge_kernel,
        out_shape=jax.ShapeDtypeStruct(parts.shape[1:], jnp.bfloat16),
        in_specs=[vmem] * 2,
        out_specs=vmem,
        compiler_params=pltpu.CompilerParams(vmem_limit_bytes=40 * MIB),
        name="merge",
    )(parts, lse)


def inverse_of(migration):
    slot_ids = jnp.arange(migration.shape[0], dtype=jnp.int32)
    return jnp.sum(jnp.where(migration[None, :] == slot_ids[:, None], slot_ids[None, :], 0), axis=1)


def per_device(
    step_inputs,
    attention_gain,
    query_weight,
    key_value_weight,
    output_weight,
    prompt_cache,
    page_table,
    cache_lengths,
    migration,
    parents,
    routes,
    feedforward_gain,
    router_weight,
    expert_gate,
    expert_up,
    expert_down,
    shared_gate,
    shared_up,
    shared_down,
):
    n_req = lax.axis_size("req")
    n_blk = lax.axis_size("blk")
    req_index = lax.axis_index("req")
    blk_index = lax.axis_index("blk")
    steps, rows_dev, width_local = step_inputs.shape
    rows = steps * rows_dev
    _, pages_local, page_length, features = prompt_cache.shape
    model_width = width_local * n_blk
    slices_dev = expert_gate.shape[0]
    hidden_dev = expert_gate.shape[2]
    split_count = FFE // hidden_dev
    inverse = inverse_of(migration)

    here = step_inputs.reshape(rows, width_local)
    padded = jnp.pad(parents, ((0, 0), (0, -parents.shape[1] % HEAD_WIDTH)))
    normed_x, x_local, all_parents = route_rows(here, migration, attention_gain, 0, (padded,))
    my_parents = lax.dynamic_index_in_dim(all_parents, migration[req_index], 0, False)[
        :, : parents.shape[1]
    ]
    q_local = jnp.dot(normed_x, query_weight, preferred_element_type=jnp.float32)
    kv_local = jnp.dot(normed_x, key_value_weight, preferred_element_type=jnp.float32)
    q_blocks, kv_blocks = push(
        [q_local.astype(jnp.bfloat16), kv_local.astype(jnp.bfloat16)], "blk", 3, gather=True
    )
    q = jnp.transpose(q_blocks, (1, 0, 2)).reshape(rows, -1)
    kv = jnp.transpose(kv_blocks, (1, 0, 2)).reshape(rows, -1)

    length = cache_lengths[req_index]
    half = HEAD_WIDTH // 2
    frequency = rope_base ** (-2.0 * jnp.arange(half, dtype=jnp.float32) / HEAD_WIDTH)
    positions = length + jnp.arange(rows, dtype=jnp.int32) // rows_dev
    angles = positions.astype(jnp.float32)[:, None] * frequency
    cosines, sines = jnp.cos(angles), jnp.sin(angles)
    cosines = jnp.concatenate([cosines, cosines], axis=1)
    sines = jnp.concatenate([-sines, sines], axis=1)
    row_ids = jnp.arange(rows, dtype=jnp.int32)
    parent_rows = jnp.concatenate(
        [
            jnp.full((rows_dev,), -1, jnp.int32),
            jnp.arange(rows_dev, dtype=jnp.int32) // BEAMS * BEAMS + my_parents[0],
        ]
    )
    parent = (parent_rows[:, None] == row_ids[None, :]).astype(jnp.bfloat16)
    table = lax.dynamic_index_in_dim(page_table, req_index, 0, False)[0]
    local_ids = jnp.arange(pages_local, dtype=jnp.int32)
    logical = jnp.sum(jnp.where(table[None, :] == local_ids[:, None], local_ids[None, :], 0), axis=1)
    key_positions = (
        (logical * n_blk + blk_index)[:, None] * page_length
        + jnp.arange(page_length, dtype=jnp.int32)[None, :]
    ).reshape(1, -1)
    tail = jnp.stack([(blk_index == 0).astype(jnp.int32), length])
    part, lse = attention_part(
        tail,
        q,
        kv,
        parent,
        cosines,
        sines,
        key_positions,
        prompt_cache.reshape(pages_local * page_length, features),
    )
    share = rows // n_blk
    parts, lses = push(
        [part.reshape(n_blk, share, -1), lse.reshape(n_blk, share, HEAD_WIDTH)], "blk", 4
    )
    heads_mine = merge(parts, lses)
    (heads,) = push([heads_mine], "blk", 5, gather=True)
    heads = heads.reshape(rows, -1)
    attended_there = (
        x_local.astype(jnp.float32)
        + jnp.dot(heads, output_weight, preferred_element_type=jnp.float32)
    ).astype(jnp.bfloat16)
    normed_h, attended_local = route_rows(attended_there, inverse, feedforward_gain, 6)

    room = steps * CAP
    slice_ids = (
        jnp.arange(n_req, dtype=jnp.int32)[:, None] * n_blk + blk_index
    ) * slices_dev + jnp.arange(slices_dev, dtype=jnp.int32)[None, :]
    targets = (slice_ids // split_count).reshape(-1)
    chosen = routes.reshape(rows, TOPK)
    named = jnp.any(chosen[:, :, None] == jnp.arange(E, dtype=jnp.int32), axis=1)
    match = jnp.any(chosen[None] == targets[:, None, None], axis=-1)
    below = (row_ids[:, None] <= row_ids[None, :]).astype(jnp.bfloat16)
    places = jnp.dot(
        match.astype(jnp.bfloat16), below, preferred_element_type=jnp.float32
    ).astype(jnp.int32)
    places = jnp.where(match, places - 1, -1)
    taken = places[:, None, :] == jnp.arange(room, dtype=jnp.int32)[None, :, None]
    dispatch = taken.reshape(-1, rows)
    sending = (
        jnp.dot(dispatch.astype(jnp.bfloat16), normed_h, preferred_element_type=jnp.float32)
        .astype(jnp.bfloat16)
        .reshape(n_req, slices_dev * room, model_width)
    )
    logits = jnp.dot(normed_h, router_weight, preferred_element_type=jnp.float32)
    raised = jnp.where(named, jnp.exp(jnp.where(named, logits, 0.0)), 0.0)
    gates = raised / jnp.sum(raised, axis=1, keepdims=True)
    expert_of = (targets[:, None] == jnp.arange(E, dtype=jnp.int32)).astype(jnp.float32)
    gate_of = jnp.dot(gates, expert_of.T, precision=lax.Precision.HIGHEST)
    mixing = jnp.where(
        jnp.transpose(taken, (2, 0, 1)), gate_of[:, :, None], 0.0
    ).reshape(rows, -1)
    high = mixing.astype(jnp.bfloat16)
    low = (mixing - high.astype(jnp.float32)).astype(jnp.bfloat16)
    blocks = run_experts(
        sending,
        (expert_gate, expert_up, expert_down),
        (shared_gate, shared_up, shared_down),
        high,
        low,
        normed_h,
        n_blk,
        9,
    )
    (blocks,) = push([blocks], "blk", 11)
    summed = jnp.sum(blocks.astype(jnp.float32), axis=0)
    out = (attended_local.astype(jnp.float32) + summed).astype(jnp.bfloat16)
    return out.reshape(steps, rows_dev, width_local)


def solution(mesh):
    in_specs = (
        P(None, "req", "blk"),
        P(),
        P(None, "blk"),
        P(None, "blk"),
        P(None, "blk"),
        P("req", "blk", None, None),
        P(None, "blk", None),
        P(),
        P(),
        P(None, "req"),
        P(None, "req", None),
        P(),
        P(),
        P(("req", "blk"), None, None),
        P(("req", "blk"), None, None),
        P(("req", "blk"), None, None),
        P(None, "blk"),
        P(None, "blk"),
        P("blk", None),
    )
    out_specs = P(None, "req", "blk")
    return jax.shard_map(
        per_device, mesh=mesh, in_specs=in_specs, out_specs=out_specs, check_vma=False
    )
```

```python
import functools

import jax
import jax.numpy as jnp
from jax import lax
from jax.experimental import pallas as pl
from jax.experimental.pallas import tpu as pltpu
from jax.sharding import PartitionSpec as P

QUERY_HEADS = 20
KEY_VALUE_HEADS = 4
HEAD_WIDTH = 128
E = 64
FFE = 1536
TOPK = 6
BEAMS = 8
CAP = 16
GROUP = QUERY_HEADS // KEY_VALUE_HEADS

epsilon = 1e-05
rope_base = 500000.0
masked_floor = -1e30
MIB = 1 << 20


def push_kernel(axis, n, count, gather, *refs):
    ins, outs = refs[:count], refs[count : 2 * count]
    send_sem, recv_sem, local_sem = refs[2 * count :]
    me = lax.axis_index(axis)
    barrier = pltpu.get_barrier_semaphore()
    for k in range(1, n):
        pl.semaphore_signal(
            barrier,
            inc=1,
            device_id={axis: lax.rem(me + k, n)},
            device_id_type=pl.DeviceIdType.MESH,
        )
    pl.semaphore_wait(barrier, n - 1)
    copies = []
    for k in range(1, n):
        to = lax.rem(me + k, n)
        for i in range(count):
            copy = pltpu.make_async_remote_copy(
                src_ref=ins[i] if gather[i] else ins[i].at[to],
                dst_ref=outs[i].at[me],
                send_sem=send_sem.at[i, k],
                recv_sem=recv_sem.at[i, k],
                device_id={axis: to},
                device_id_type=pl.DeviceIdType.MESH,
            )
            copy.start()
            copies.append(copy)
    own = []
    for i in range(count):
        copy = pltpu.make_async_copy(
            ins[i] if gather[i] else ins[i].at[me], outs[i].at[me], local_sem.at[i]
        )
        copy.start()
        own.append(copy)
    for copy in own:
        copy.wait()
    for copy in copies:
        copy.wait()


def push(arrays, axis, collective_id, gather=False):
    n = lax.axis_size(axis)
    count = len(arrays)
    if not isinstance(gather, tuple):
        gather = (gather,) * count
    shapes = [
        jax.ShapeDtypeStruct(((n,) + a.shape) if whole else a.shape, a.dtype)
        for a, whole in zip(arrays, gather)
    ]
    return pl.pallas_call(
        functools.partial(push_kernel, axis, n, count, gather),
        out_shape=shapes,
        in_specs=[pl.BlockSpec(memory_space=pl.ANY)] * count,
        out_specs=[pl.BlockSpec(memory_space=pl.ANY)] * count,
        scratch_shapes=[
            pltpu.SemaphoreType.DMA((count, n)),
            pltpu.SemaphoreType.DMA((count, n)),
            pltpu.SemaphoreType.DMA((count,)),
        ],
        compiler_params=pltpu.CompilerParams(collective_id=collective_id, has_side_effects=True),
        name=f"push_{axis}_{collective_id}",
    )(*arrays)


def route_kernel(n, n_blk, extra, block_for, gain_ref, pieces, *refs):
    besides, refs = refs[:extra], refs[extra:]
    normed_ref, rows_ref, *refs = refs
    gathered, refs = refs[:extra], refs[extra:]
    spread, staged, landed, wide, hop_send, hop_recv, local_sem = refs
    me, blk = lax.axis_index("req"), lax.axis_index("blk")
    barrier = pltpu.get_barrier_semaphore()

    def at(axis, k):
        here, size = (me, n) if axis == "req" else (blk, n_blk)
        return {axis: lax.rem(here + k, size)}

    partners = [("req", k) for k in range(1, n)] + [("blk", k) for k in range(1, n_blk)]
    for axis, k in partners:
        pl.semaphore_signal(
            barrier, inc=1, device_id=at(axis, k), device_id_type=pl.DeviceIdType.MESH
        )
    pl.semaphore_wait(barrier, len(partners))

    def send(source, landing, phase, axis, k):
        copy = pltpu.make_async_remote_copy(
            src_ref=source,
            dst_ref=landing,
            send_sem=hop_send.at[phase, k],
            recv_sem=hop_recv.at[phase, k],
            device_id=at(axis, k),
            device_id_type=pl.DeviceIdType.MESH,
        )
        copy.start()
        return copy

    def keep(source, landing, number):
        copy = pltpu.make_async_copy(source, landing, local_sem.at[number])
        copy.start()
        return copy

    copies = [
        send(pieces.at[lax.rem(me + k, n)], spread.at[me], 0, "req", k) for k in range(1, n)
    ]
    copies.append(keep(pieces.at[me], spread.at[me], 0))
    late = []
    for i in range(extra):
        late += [send(besides[i], gathered[i].at[me], 3 + i, "req", k) for k in range(1, n)]
        late.append(keep(besides[i], gathered[i].at[me], 3 + i))
    for copy in copies:
        copy.wait()
    for d in range(n):
        staged[d] = spread[block_for[d]]
    copies = [
        send(staged.at[lax.rem(me + k, n)], landed.at[me], 1, "req", k) for k in range(1, n)
    ]
    copies.append(keep(staged.at[me], landed.at[me], 1))
    for copy in copies:
        copy.wait()
    copies = [send(landed, wide.at[blk], 2, "blk", k) for k in range(1, n_blk)]
    copies.append(keep(landed, wide.at[blk], 2))
    rows_ref[...] = landed[...]
    for copy in copies + late:
        copy.wait()
    rows, model = normed_ref.shape
    width = model // n_blk
    blocks = [wide[b].astype(jnp.float32).reshape(rows, width) for b in range(n_blk)]
    squares = jnp.sum(blocks[0] * blocks[0], axis=1, keepdims=True)
    for block in blocks[1:]:
        squares += jnp.sum(block * block, axis=1, keepdims=True)
    inverse = lax.rsqrt(squares / model + epsilon)
    for b in range(n_blk):
        columns = slice(b * width, (b + 1) * width)
        normed_ref[:, columns] = (blocks[b] * inverse * gain_ref[:, columns]).astype(jnp.bfloat16)


def route_rows(rows, block_for, gain, collective_id, beside=()):
    n, n_blk = lax.axis_size("req"), lax.axis_size("blk")
    count, width = rows.shape
    extra = len(beside)
    pieces = rows.reshape(n, count // n, width)
    anywhere = pl.BlockSpec(memory_space=pl.ANY)
    vmem = pl.BlockSpec(memory_space=pltpu.VMEM)
    phases = 3 + extra
    hops = max(n, n_blk)
    normed, arrived, *gathered = pl.pallas_call(
        functools.partial(route_kernel, n, n_blk, extra),
        out_shape=[
            jax.ShapeDtypeStruct((count, width * n_blk), jnp.bfloat16),
            jax.ShapeDtypeStruct(pieces.shape, rows.dtype),
        ]
        + [jax.ShapeDtypeStruct((n,) + a.shape, a.dtype) for a in beside],
        in_specs=[pl.BlockSpec(memory_space=pltpu.SMEM), vmem, vmem] + [anywhere] * extra,
        out_specs=[vmem] * 2 + [anywhere] * extra,
        scratch_shapes=[pltpu.VMEM(pieces.shape, rows.dtype)] * 3
        + [
            pltpu.VMEM((n_blk,) + pieces.shape, rows.dtype),
            pltpu.SemaphoreType.DMA((phases, hops)),
            pltpu.SemaphoreType.DMA((phases, hops)),
            pltpu.SemaphoreType.DMA((phases,)),
        ],
        compiler_params=pltpu.CompilerParams(
            collective_id=collective_id, has_side_effects=True, vmem_limit_bytes=32 * MIB
        ),
        name=f"route_{collective_id}",
    )(block_for, gain.reshape(1, -1), pieces, *beside)
    return (normed, arrived.reshape(rows.shape), *gathered)


def experts_kernel(
    n, sending, gate_hbm, up_hbm, down_hbm, shared_gate, shared_up, shared_down,
    high_ref, low_ref, normed_ref, out_ref,
    gate, up, down, held, hidden, back, shared_act, shared_ref,
    weight_sem, send_sem, recv_sem, home_sem, back_sem, own_sem, *apart,
):
    me = lax.axis_index("req")
    near = n // 2
    mine = lax.rem(me, near)
    base = me - mine
    other = lax.rem(base + near, n)

    def target(i):
        return (base if i < near else other) + lax.rem(mine + i % near, near)

    def source(i):
        return (base if i < near else other) + lax.rem(mine + near - i % near, near)

    slices, _, width = gate.shape
    room = held.shape[1] // slices
    last = slices - 1
    shared_width = shared_gate.shape[1]
    if apart:
        places = apart
    else:
        columns = pl.ds(0, shared_width)
        places = (gate.at[last, :, columns], up.at[last, :, columns], down.at[last, columns, :])
    shared_copies = [
        pltpu.make_async_copy(hbm, vmem, weight_sem.at[3 * slices + number])
        for number, (hbm, vmem) in enumerate(zip((shared_gate, shared_up, shared_down), places))
    ]
    weights = [
        pltpu.make_async_copy(hbm.at[j], vmem.at[j], weight_sem.at[3 * j + number])
        for j in range(slices)
        for number, (hbm, vmem) in enumerate(((gate_hbm, gate), (up_hbm, up), (down_hbm, down)))
    ]
    for copy in shared_copies + weights[: 3 * last]:
        copy.start()

    barrier = pltpu.get_barrier_semaphore()
    for k in range(1, n):
        pl.semaphore_signal(
            barrier,
            inc=1,
            device_id={"req": lax.rem(me + k, n)},
            device_id_type=pl.DeviceIdType.MESH,
        )
    pl.semaphore_wait(barrier, n - 1)

    there, home = {}, {}
    for i in list(range(near, n)) + list(range(1, near)):
        there[i] = pltpu.make_async_remote_copy(
            src_ref=sending.at[target(i)],
            dst_ref=held.at[i],
            send_sem=send_sem.at[i],
            recv_sem=recv_sem.at[i],
            device_id={"req": target(i)},
            device_id_type=pl.DeviceIdType.MESH,
        )
        there[i].start()
    own = pltpu.make_async_copy(sending.at[me], held.at[0], own_sem.at[0])
    own.start()

    tile = 256 if width % 256 == 0 else 128
    model = down.shape[2]
    wide = 512

    for copy in shared_copies:
        copy.wait()
    step = 256 if shared_width % 256 == 0 else shared_width
    for f in range(0, shared_width, step):
        at = slice(f, f + step)
        g = jnp.dot(normed_ref[...], places[0][:, at], preferred_element_type=jnp.float32)
        u = jnp.dot(normed_ref[...], places[1][:, at], preferred_element_type=jnp.float32)
        shared_act[:, at] = (g / (1.0 + jnp.exp(-g)) * u).astype(jnp.bfloat16)
    for c in range(0, model, wide):
        at = slice(c, c + wide)
        shared_ref[:, at] = jnp.dot(
            shared_act[...], places[2][:, at], preferred_element_type=jnp.float32
        )
    for copy in weights[3 * last :]:
        copy.start()

    def chunk(first, last, wait_weights):
        count = last - first
        for i in range(first, last):
            if i == 0:
                own.wait()
            else:
                there[i].wait_recv()
        for j in range(slices):
            rows_at = pl.ds(j * room, room)
            if wait_weights:
                weights[3 * j].wait()
                weights[3 * j + 1].wait()

            @pl.loop(0, width // tile)
            def _(f):
                at = pl.ds(pl.multiple_of(f * tile, tile), tile)
                rows = held[first:last, rows_at, :].reshape(count * room, model)
                g = jnp.dot(rows, gate[j, :, at], preferred_element_type=jnp.float32)
                u = jnp.dot(rows, up[j, :, at], preferred_element_type=jnp.float32)
                hidden[: count * room, at] = (g / (1.0 + jnp.exp(-g)) * u).astype(jnp.bfloat16)

            if wait_weights:
                weights[3 * j + 2].wait()

            @pl.loop(0, model // wide)
            def _(c):
                at = pl.ds(pl.multiple_of(c * wide, wide), wide)
                produced = jnp.dot(
                    hidden[: count * room, :], down[j, :, at], preferred_element_type=jnp.float32
                )
                held[first:last, rows_at, at] = produced.astype(jnp.bfloat16).reshape(
                    count, room, wide
                )

        for i in range(first, last):
            if i == 0:
                continue
            home[i] = pltpu.make_async_remote_copy(
                src_ref=held.at[i],
                dst_ref=back.at[me],
                send_sem=home_sem.at[i],
                recv_sem=back_sem.at[i],
                device_id={"req": source(i)},
                device_id_type=pl.DeviceIdType.MESH,
            )
            home[i].start()

    chunk(0, near, True)
    own_back = pltpu.make_async_copy(held.at[0], back.at[me], own_sem.at[1])
    own_back.start()
    chunk(near, near + near // 2, False)
    chunk(near + near // 2, n, False)
    own_back.wait()
    for i in range(1, n):
        there[i].wait_send()
        home[i].wait()
    block = out_ref.shape[2]
    returned = back[...].reshape(-1, model)
    for b in range(out_ref.shape[0]):
        at = pl.ds(b * block, block)
        part = returned[:, b * block : (b + 1) * block]
        routed = jnp.dot(high_ref[...], part, preferred_element_type=jnp.float32) + jnp.dot(
            low_ref[...], part, preferred_element_type=jnp.float32
        )
        out_ref[b] = (routed + shared_ref[:, at]).astype(jnp.bfloat16)


def run_experts(sending, experts, shared, high, low, normed, n_blk, collective_id):
    n, taken, model = sending.shape
    gate, up, down = experts
    slices, _, width = gate.shape
    rows = normed.shape[0]
    shared_width = shared[0].shape[1]
    fits = shared_width % HEAD_WIDTH == 0 and shared_width <= width
    apart = [] if fits else [pltpu.VMEM(a.shape, a.dtype) for a in shared]
    anywhere = pl.BlockSpec(memory_space=pl.ANY)
    vmem = pl.BlockSpec(memory_space=pltpu.VMEM)
    return pl.pallas_call(
        functools.partial(experts_kernel, n),
        out_shape=jax.ShapeDtypeStruct((n_blk, rows, model // n_blk), jnp.bfloat16),
        in_specs=[anywhere] * 7 + [vmem] * 3,
        out_specs=vmem,
        scratch_shapes=[
            pltpu.VMEM(gate.shape, gate.dtype),
            pltpu.VMEM(up.shape, up.dtype),
            pltpu.VMEM(down.shape, down.dtype),
            pltpu.VMEM((n, taken, model), jnp.bfloat16),
            pltpu.VMEM((n // 2 * taken // slices, width), jnp.bfloat16),
            pltpu.VMEM((n, taken, model), jnp.bfloat16),
            pltpu.VMEM((rows, shared_width), jnp.bfloat16),
            pltpu.VMEM((rows, model), jnp.float32),
            pltpu.SemaphoreType.DMA((3 * slices + 3,)),
            pltpu.SemaphoreType.DMA((n,)),
            pltpu.SemaphoreType.DMA((n,)),
            pltpu.SemaphoreType.DMA((n,)),
            pltpu.SemaphoreType.DMA((n,)),
            pltpu.SemaphoreType.DMA((2,)),
            *apart,
        ],
        compiler_params=pltpu.CompilerParams(
            collective_id=collective_id, has_side_effects=True, vmem_limit_bytes=60 * MIB
        ),
        name="experts",
    )(sending, *experts, *shared, high, low, normed)


def attention_kernel(
    tail_ref, q_ref, kv_ref, parent_ref, cos_ref, sin_ref, pos_ref, cache_ref, o_ref, lse_ref
):
    rows = q_ref.shape[0]
    scaling = HEAD_WIDTH ** (-0.5)
    key_width = KEY_VALUE_HEADS * HEAD_WIDTH
    cosines, sines = cos_ref[...], sin_ref[...]

    def rotated(block):
        block = block.astype(jnp.float32)
        half = HEAD_WIDTH // 2
        swapped = jnp.concatenate([block[:, half:], block[:, :half]], axis=1)
        return (block * cosines + swapped * sines).astype(jnp.bfloat16)

    tails_here = tail_ref[0] > 0
    valid = pos_ref[...] < tail_ref[1]
    parent = parent_ref[...]
    has_parent = jnp.sum(parent.astype(jnp.float32), axis=1, keepdims=True) > 0.5
    lse_ref[...] = jnp.full(lse_ref.shape, masked_floor, jnp.float32)
    for kv_head in range(KEY_VALUE_HEADS):
        keys_at = pl.ds(kv_head * HEAD_WIDTH, HEAD_WIDTH)
        values_at = pl.ds(key_width + kv_head * HEAD_WIDTH, HEAD_WIDTH)
        own_key = rotated(kv_ref[:, keys_at])
        own_value = kv_ref[:, values_at]
        parent_key = jnp.dot(parent, own_key, preferred_element_type=jnp.float32)
        parent_value = jnp.dot(parent, own_value, preferred_element_type=jnp.float32)
        own_key = own_key.astype(jnp.float32)
        own_value = own_value.astype(jnp.float32)
        keys = cache_ref[:, keys_at]
        values = cache_ref[:, values_at]
        for g in range(GROUP):
            head = kv_head * GROUP + g
            at = pl.ds(head * HEAD_WIDTH, HEAD_WIDTH)
            query = rotated(q_ref[:, at])
            scores = (
                lax.dot_general(
                    query, keys, (((1,), (1,)), ((), ())), preferred_element_type=jnp.float32
                )
                * scaling
            )
            query = query.astype(jnp.float32)
            own = jnp.sum(query * own_key, axis=1, keepdims=True) * scaling
            par = jnp.sum(query * parent_key, axis=1, keepdims=True) * scaling
            own = jnp.where(tails_here, own, masked_floor)
            par = jnp.where(has_parent & tails_here, par, masked_floor)
            scores = jnp.where(valid, scores, masked_floor)
            peak = jnp.maximum(jnp.max(scores, axis=1, keepdims=True), jnp.maximum(own, par))
            probs = jnp.where(valid, jnp.exp(scores - peak), 0.0)
            own = jnp.where(tails_here, jnp.exp(own - peak), 0.0)
            par = jnp.where(has_parent & tails_here, jnp.exp(par - peak), 0.0)
            total = jnp.sum(probs, axis=1, keepdims=True) + own + par
            weighted = jnp.dot(
                probs.astype(jnp.bfloat16), values, preferred_element_type=jnp.float32
            )
            weighted += own.astype(jnp.bfloat16).astype(jnp.float32) * own_value
            weighted += par.astype(jnp.bfloat16).astype(jnp.float32) * parent_value
            live = total > 0.0
            safe = jnp.where(live, total, 1.0)
            o_ref[:, at] = (weighted / safe).astype(jnp.bfloat16)
            lse_ref[:, head : head + 1] = jnp.where(live, peak + jnp.log(safe), masked_floor)


def attention_part(tail, q, kv, parent, cosines, sines, positions, cache):
    rows = q.shape[0]
    vmem = pl.BlockSpec(memory_space=pltpu.VMEM)
    return pl.pallas_call(
        attention_kernel,
        out_shape=[
            jax.ShapeDtypeStruct(q.shape, jnp.bfloat16),
            jax.ShapeDtypeStruct((rows, HEAD_WIDTH), jnp.float32),
        ],
        in_specs=[pl.BlockSpec(memory_space=pltpu.SMEM)] + [vmem] * 7,
        out_specs=[vmem] * 2,
        compiler_params=pltpu.CompilerParams(vmem_limit_bytes=40 * MIB),
        name="attention_part",
    )(tail, q, kv, parent, cosines, sines, positions, cache)


def merge_kernel(n, part_ref, lse_part_ref, out_ref, o_ref, lse_ref, mine, send_sem, recv_sem, own_sem):
    me = lax.axis_index("blk")
    barrier = pltpu.get_barrier_semaphore()
    partners = [lax.rem(me + k, n) for k in range(1, n)]
    for to in partners:
        pl.semaphore_signal(
            barrier, inc=1, device_id={"blk": to}, device_id_type=pl.DeviceIdType.MESH
        )
    pl.semaphore_wait(barrier, n - 1)

    def spread(phase, source, landing, whole):
        copies = [
            pltpu.make_async_remote_copy(
                src_ref=source if whole else source.at[to],
                dst_ref=landing.at[me],
                send_sem=send_sem.at[phase, k],
                recv_sem=recv_sem.at[phase, k],
                device_id={"blk": to},
                device_id_type=pl.DeviceIdType.MESH,
            )
            for k, to in enumerate(partners)
        ]
        copies.append(
            pltpu.make_async_copy(
                source if whole else source.at[me], landing.at[me], own_sem.at[phase]
            )
        )
        for copy in copies:
            copy.start()
        return copies

    for copy in spread(0, part_ref, o_ref, False) + spread(1, lse_part_ref, lse_ref, False):
        copy.wait()
    peaks = lse_ref[0]
    for b in range(1, n):
        peaks = jnp.maximum(peaks, lse_ref[b])
    scales = [jnp.exp(lse_ref[b] - peaks) for b in range(n)]
    total = scales[0]
    for b in range(1, n):
        total = total + scales[b]
    scales = [scale / total for scale in scales]
    for head in range(QUERY_HEADS):
        at = pl.ds(head * HEAD_WIDTH, HEAD_WIDTH)
        acc = o_ref[0, :, at].astype(jnp.float32) * scales[0][:, head : head + 1]
        for b in range(1, n):
            acc += o_ref[b, :, at].astype(jnp.float32) * scales[b][:, head : head + 1]
        mine[:, at] = acc.astype(jnp.bfloat16)
    for copy in spread(2, mine, out_ref, True):
        copy.wait()


def merge(part, lse, collective_id):
    n = part.shape[0]
    vmem = pl.BlockSpec(memory_space=pltpu.VMEM)
    return pl.pallas_call(
        functools.partial(merge_kernel, n),
        out_shape=jax.ShapeDtypeStruct(part.shape, jnp.bfloat16),
        in_specs=[vmem] * 2,
        out_specs=vmem,
        scratch_shapes=[
            pltpu.VMEM(part.shape, part.dtype),
            pltpu.VMEM(lse.shape, lse.dtype),
            pltpu.VMEM(part.shape[1:], jnp.bfloat16),
            pltpu.SemaphoreType.DMA((3, n)),
            pltpu.SemaphoreType.DMA((3, n)),
            pltpu.SemaphoreType.DMA((3,)),
        ],
        compiler_params=pltpu.CompilerParams(
            collective_id=collective_id, has_side_effects=True, vmem_limit_bytes=40 * MIB
        ),
        name="merge",
    )(part, lse)


def inverse_of(migration):
    slot_ids = jnp.arange(migration.shape[0], dtype=jnp.int32)
    return jnp.sum(jnp.where(migration[None, :] == slot_ids[:, None], slot_ids[None, :], 0), axis=1)


def per_device(
    step_inputs,
    attention_gain,
    query_weight,
    key_value_weight,
    output_weight,
    prompt_cache,
    page_table,
    cache_lengths,
    migration,
    parents,
    routes,
    feedforward_gain,
    router_weight,
    expert_gate,
    expert_up,
    expert_down,
    shared_gate,
    shared_up,
    shared_down,
):
    n_req = lax.axis_size("req")
    n_blk = lax.axis_size("blk")
    req_index = lax.axis_index("req")
    blk_index = lax.axis_index("blk")
    steps, rows_dev, width_local = step_inputs.shape
    rows = steps * rows_dev
    _, pages_local, page_length, features = prompt_cache.shape
    model_width = width_local * n_blk
    slices_dev = expert_gate.shape[0]
    hidden_dev = expert_gate.shape[2]
    split_count = FFE // hidden_dev
    inverse = inverse_of(migration)

    here = step_inputs.reshape(rows, width_local)
    padded = jnp.pad(parents, ((0, 0), (0, -parents.shape[1] % HEAD_WIDTH)))
    normed_x, x_local, all_parents = route_rows(here, migration, attention_gain, 0, (padded,))
    my_parents = lax.dynamic_index_in_dim(all_parents, migration[req_index], 0, False)[
        :, : parents.shape[1]
    ]
    q_local = jnp.dot(normed_x, query_weight, preferred_element_type=jnp.float32)
    kv_local = jnp.dot(normed_x, key_value_weight, preferred_element_type=jnp.float32)
    q_blocks, kv_blocks = push(
        [q_local.astype(jnp.bfloat16), kv_local.astype(jnp.bfloat16)], "blk", 3, gather=True
    )
    q = jnp.transpose(q_blocks, (1, 0, 2)).reshape(rows, -1)
    kv = jnp.transpose(kv_blocks, (1, 0, 2)).reshape(rows, -1)

    length = cache_lengths[req_index]
    half = HEAD_WIDTH // 2
    frequency = rope_base ** (-2.0 * jnp.arange(half, dtype=jnp.float32) / HEAD_WIDTH)
    positions = length + jnp.arange(rows, dtype=jnp.int32) // rows_dev
    angles = positions.astype(jnp.float32)[:, None] * frequency
    cosines, sines = jnp.cos(angles), jnp.sin(angles)
    cosines = jnp.concatenate([cosines, cosines], axis=1)
    sines = jnp.concatenate([-sines, sines], axis=1)
    row_ids = jnp.arange(rows, dtype=jnp.int32)
    parent_rows = jnp.concatenate(
        [
            jnp.full((rows_dev,), -1, jnp.int32),
            jnp.arange(rows_dev, dtype=jnp.int32) // BEAMS * BEAMS + my_parents[0],
        ]
    )
    parent = (parent_rows[:, None] == row_ids[None, :]).astype(jnp.bfloat16)
    table = lax.dynamic_index_in_dim(page_table, req_index, 0, False)[0]
    local_ids = jnp.arange(pages_local, dtype=jnp.int32)
    logical = jnp.sum(jnp.where(table[None, :] == local_ids[:, None], local_ids[None, :], 0), axis=1)
    key_positions = (
        (logical * n_blk + blk_index)[:, None] * page_length
        + jnp.arange(page_length, dtype=jnp.int32)[None, :]
    ).reshape(1, -1)
    tail = jnp.stack([(blk_index == 0).astype(jnp.int32), length])
    part, lse = attention_part(
        tail,
        q,
        kv,
        parent,
        cosines,
        sines,
        key_positions,
        prompt_cache.reshape(pages_local * page_length, features),
    )
    share = rows // n_blk
    heads = merge(part.reshape(n_blk, share, -1), lse.reshape(n_blk, share, HEAD_WIDTH), 4)
    heads = heads.reshape(rows, -1)
    attended_there = (
        x_local.astype(jnp.float32)
        + jnp.dot(heads, output_weight, preferred_element_type=jnp.float32)
    ).astype(jnp.bfloat16)
    normed_h, attended_local = route_rows(attended_there, inverse, feedforward_gain, 6)

    room = steps * CAP
    slice_ids = (
        jnp.arange(n_req, dtype=jnp.int32)[:, None] * n_blk + blk_index
    ) * slices_dev + jnp.arange(slices_dev, dtype=jnp.int32)[None, :]
    targets = (slice_ids // split_count).reshape(-1)
    chosen = routes.reshape(rows, TOPK)
    named = jnp.any(chosen[:, :, None] == jnp.arange(E, dtype=jnp.int32), axis=1)
    match = jnp.any(chosen[None] == targets[:, None, None], axis=-1)
    below = (row_ids[:, None] <= row_ids[None, :]).astype(jnp.bfloat16)
    places = jnp.dot(
        match.astype(jnp.bfloat16), below, preferred_element_type=jnp.float32
    ).astype(jnp.int32)
    places = jnp.where(match, places - 1, -1)
    taken = places[:, None, :] == jnp.arange(room, dtype=jnp.int32)[None, :, None]
    dispatch = taken.reshape(-1, rows)
    sending = (
        jnp.dot(dispatch.astype(jnp.bfloat16), normed_h, preferred_element_type=jnp.float32)
        .astype(jnp.bfloat16)
        .reshape(n_req, slices_dev * room, model_width)
    )
    logits = jnp.dot(normed_h, router_weight, preferred_element_type=jnp.float32)
    raised = jnp.where(named, jnp.exp(jnp.where(named, logits, 0.0)), 0.0)
    gates = raised / jnp.sum(raised, axis=1, keepdims=True)
    expert_of = (targets[:, None] == jnp.arange(E, dtype=jnp.int32)).astype(jnp.float32)
    gate_of = jnp.dot(gates, expert_of.T, precision=lax.Precision.HIGHEST)
    mixing = jnp.where(
        jnp.transpose(taken, (2, 0, 1)), gate_of[:, :, None], 0.0
    ).reshape(rows, -1)
    high = mixing.astype(jnp.bfloat16)
    low = (mixing - high.astype(jnp.float32)).astype(jnp.bfloat16)
    blocks = run_experts(
        sending,
        (expert_gate, expert_up, expert_down),
        (shared_gate, shared_up, shared_down),
        high,
        low,
        normed_h,
        n_blk,
        9,
    )
    (blocks,) = push([blocks], "blk", 11)
    summed = jnp.sum(blocks.astype(jnp.float32), axis=0)
    out = (attended_local.astype(jnp.float32) + summed).astype(jnp.bfloat16)
    return out.reshape(steps, rows_dev, width_local)


def solution(mesh):
    in_specs = (
        P(None, "req", "blk"),
        P(),
        P(None, "blk"),
        P(None, "blk"),
        P(None, "blk"),
        P("req", "blk", None, None),
        P(None, "blk", None),
        P(),
        P(),
        P(None, "req"),
        P(None, "req", None),
        P(),
        P(),
        P(("req", "blk"), None, None),
        P(("req", "blk"), None, None),
        P(("req", "blk"), None, None),
        P(None, "blk"),
        P(None, "blk"),
        P("blk", None),
    )
    out_specs = P(None, "req", "blk")
    return jax.shard_map(
        per_device, mesh=mesh, in_specs=in_specs, out_specs=out_specs, check_vma=False
    )
```
